512 devices in a mesh: seg: 128 (over y, z, core), rep: 4 (over x).
Axes of the slice: x: 4, y: 4, z: 16, core: 2. Of those that a mesh axis runs over, the one named last changes fastest.
Arguments:
- currents: float32 [32, 786432], P('rep', 'seg'), may hold values from -6 to 6
- requested: int32 [128, 4, 128, 2], P('seg', 'rep'), may hold values from -1 to 47, as said below
- block_rows: int32 [128, 4, 128], P('seg', 'rep'), may hold values from 0 to 6143, as said below
- block_slots: int32 [128, 4, 128], P('seg', 'rep'), may hold values from 0 to 255, as said below
- coupling: bfloat16 [128, 4, 128, 128, 128], P('seg', 'rep'), may hold values from -0.15625 to 0.15625
Outputs:
- voltages: float32 [32, 786432], P('rep', 'seg')
The draws below stay inside these ranges and needn't reach their ends.
Inputs may be any that keep to these rules, and one draw needn't show every extreme that they name: `requested`: each entry is -1 or a block number whose remainder modulo 4 equals the rep index r of its second dimension; the slots of one source list the non-empty ones first and name different blocks. Every reader requests exactly 2 blocks from its own index of seg, and at most 128 blocks in all for one rep index. `block_rows`: the block rows held by device s, for every rep index, lie in s * 48 - 48 // 4 to (s + 1) * 48 + 48 // 4 - 1, taken modulo 6144. `block_slots`: every slot named is non-empty in requested, and every non-empty slot of a device is named by one or more of its nonzero blocks.
All inputs are finite; a program needn't handle non-finite values.
Results may differ from the reference program's by a relative error of at most 0.0029.
Values may be sent and summed in bfloat16 or wider, within the bound.
No kernel may reach another device: no remote copies, remote signals or barrier semaphores. Data moves between devices by JAX's collectives and lax.ppermute only.
A program may use at most 64 MiB of HBM per device.

```python
import math
import jax
import jax.numpy as jnp
from jax import lax

PORTS = 32
BS = 128
SEG_DEV = 6144
NNZ_DEV = 128
CAP = 2
BLK_DEV = 48
SEGMENTS = 786432
BLOCKS = 6144
N_SEG = 128
N_REP = 4


def sparse_plan(key):
    segs = jnp.arange(N_SEG, dtype=jnp.int32)
    margin = BLK_DEV // 4
    window = BLK_DEV + 2 * margin
    shape_three = (N_SEG, N_REP, N_SEG)
    offsets = jnp.arange(N_SEG - 1, dtype=jnp.int32)
    rank_scores = jax.random.randint(jax.random.fold_in(key, 31), (N_SEG, N_REP, N_SEG - 1), 0, 1 << 20, dtype=jnp.int32) * N_SEG + offsets[None, None, :]
    order = jnp.argsort(rank_scores, axis=-1, stable=True).astype(jnp.int32)
    ranks = jnp.argsort(order, axis=-1, stable=True).astype(jnp.int32)
    pair_kind = jax.random.randint(jax.random.fold_in(key, 32), (N_SEG, N_REP, N_SEG // 2), 0, 4, dtype=jnp.int32)
    kinds = jnp.take_along_axis(pair_kind, ranks // 2, axis=-1)
    first_member = ranks % 2 == 0
    paired = jnp.where(kinds < 2, 1, jnp.where((kinds == 2) == first_member, 2, 0))
    remote = jnp.where(ranks == N_SEG - 2, 0, paired).astype(jnp.int32)
    source_ids = segs[None, None, :]
    reader_ids = segs[:, None, None]
    distance = jnp.broadcast_to((source_ids - reader_ids) % N_SEG, shape_three).astype(jnp.int32)
    remote_at = jnp.take_along_axis(remote, jnp.maximum(distance - 1, 0), axis=-1)
    counts = jnp.where(distance == 0, 2, remote_at)
    spread = BLK_DEV // N_REP
    first_pick = jax.random.randint(jax.random.fold_in(key, 23), shape_three, 0, spread, dtype=jnp.int32)
    second_pick = (first_pick + 1 + jax.random.randint(jax.random.fold_in(key, 24), shape_three, 0, spread - 1, dtype=jnp.int32)) % spread
    rep_ids = jnp.arange(N_REP, dtype=jnp.int32)[None, :, None]
    first_block = N_REP * first_pick + rep_ids
    second_block = N_REP * second_pick + rep_ids
    requested = jnp.stack([jnp.where(counts >= 1, first_block, -1), jnp.where(counts >= 2, second_block, -1)], axis=-1).astype(jnp.int32)
    flat_live = (requested >= 0).reshape(N_SEG, N_REP, N_SEG * CAP).astype(jnp.int32)
    positions = jnp.arange(N_SEG * CAP, dtype=jnp.int32)
    scores = (1 - flat_live) * (N_SEG * CAP) + positions[None, None, :]
    ordered = jnp.argsort(scores, axis=-1, stable=True).astype(jnp.int32)
    total_live = jnp.sum(flat_live, axis=-1, keepdims=True)
    nonzero_ids = jnp.arange(NNZ_DEV, dtype=jnp.int32)[None, None, :]
    picks = nonzero_ids % total_live
    block_slots = jnp.take_along_axis(ordered, picks, axis=-1).astype(jnp.int32)
    random_rows = jax.random.randint(jax.random.fold_in(key, 25), (N_SEG, N_REP, NNZ_DEV), 0, window, dtype=jnp.int32)
    offset_rows = jnp.where(nonzero_ids < window, nonzero_ids, random_rows)
    lower_edge = segs * BLK_DEV - margin
    block_rows = ((lower_edge[:, None, None] + offset_rows + BLOCKS) % BLOCKS).astype(jnp.int32)
    return (requested, block_rows, block_slots)


def draw_requested(key, part):
    return sparse_plan(key)[0]


def draw_block_rows(key, part):
    return sparse_plan(key)[1]


def draw_block_slots(key, part):
    return sparse_plan(key)[2]


def block_levels(own_key, shape, shards, least, top_value):
    gain = 1.0
    for position, shards_of in shards:
        draws = jax.random.uniform(jax.random.fold_in(jax.random.fold_in(own_key, 6), position), (shards_of,), jnp.float32, least / len(shards), top_value / len(shards))
        gain = gain * jnp.repeat(jnp.exp(draws), shape[position] // shards_of).reshape((-1,) + (1,) * (len(shape) - 1 - position))
    return gain


def centred(stream_key, dims, width, bound, split=(), held_as=jnp.bfloat16):
    values = width * jax.random.normal(stream_key, dims, jnp.float32)
    if split:
        values = values * block_levels(stream_key, dims, split, -0.22, 0.18)
    return jnp.clip(values, -bound, bound).astype(held_as)


def setup_inputs(seed: int = 0) -> dict:
    key_list = jax.random.split(jax.random.key(seed), 6)
    return {
        "currents": centred(key_list[0], (PORTS, SEGMENTS), 1.0, 6.0, ((0, 4), (1, 128)), jnp.float32),
        "requested": draw_requested(jax.random.fold_in(key_list[5], 71), 0),
        "block_rows": draw_block_rows(jax.random.fold_in(key_list[5], 71), 0),
        "block_slots": draw_block_slots(jax.random.fold_in(key_list[5], 71), 0),
        "coupling": centred(key_list[4], (N_SEG, N_REP, NNZ_DEV, BS, BS), (BS * NNZ_DEV * N_REP // BLK_DEV) ** -0.5, 0.15625, ((0, 128), (1, 4))),
    }


ROOT_THREE = math.sqrt(3.0)
SCALE_NORM = 4.0 * math.sqrt(2.0)
LOW_PASS = ((1.0 + ROOT_THREE) / SCALE_NORM, (3.0 + ROOT_THREE) / SCALE_NORM, (3.0 - ROOT_THREE) / SCALE_NORM, (1.0 - ROOT_THREE) / SCALE_NORM)
HIGH_PASS = (LOW_PASS[3], -LOW_PASS[2], LOW_PASS[1], -LOW_PASS[0])

def reference(currents, requested, block_rows, block_slots, coupling):
    half_len = SEG_DEV // 2
    total = currents.shape[1]
    shifted = [jnp.roll(currents, -offset, axis=1)[:, 0::2] for offset in range(4)]
    low_band = LOW_PASS[0] * shifted[0] + LOW_PASS[1] * shifted[1] + LOW_PASS[2] * shifted[2] + LOW_PASS[3] * shifted[3]
    high_band = HIGH_PASS[0] * shifted[0] + HIGH_PASS[1] * shifted[1] + HIGH_PASS[2] * shifted[2] + HIGH_PASS[3] * shifted[3]
    grouped = jnp.concatenate([low_band.reshape(PORTS, N_SEG, half_len), high_band.reshape(PORTS, N_SEG, half_len)], axis=2)
    coefficients = grouped.reshape(PORTS, total).astype(jnp.bfloat16)
    vector_table = coefficients.reshape(PORTS, BLOCKS, BS)
    sources = (jnp.arange(N_SEG, dtype=jnp.int32) * BLK_DEV)[None, :, None]

    def accumulate(totals, inputs):
        wanted, rows_here, slots_here, blocks_here = inputs
        columns = (jnp.maximum(wanted, 0) + sources).astype(jnp.int32).reshape(N_REP, N_SEG * CAP)
        picked = jnp.take_along_axis(columns, slots_here, axis=1).reshape(-1)
        vectors = vector_table[:, picked, :].astype(jnp.float32)
        matrices = blocks_here.reshape(-1, BS, BS).astype(jnp.float32)
        products = jnp.einsum('nij,pnj->pni', matrices, vectors, precision=lax.Precision.HIGHEST)
        totals = totals.at[:, rows_here.reshape(-1), :].add(products)
        return (totals, None)
    start = jnp.zeros((PORTS, BLOCKS, BS), jnp.float32)
    wave_out, _ = lax.scan(accumulate, start, (requested, block_rows, block_slots, coupling))
    wave_out = wave_out.reshape(PORTS, N_SEG, 2, half_len)
    low_out = wave_out[:, :, 0, :].reshape(PORTS, total // 2)
    high_out = wave_out[:, :, 1, :].reshape(PORTS, total // 2)
    low_prev = jnp.roll(low_out, 1, axis=1)
    high_prev = jnp.roll(high_out, 1, axis=1)
    even_part = LOW_PASS[0] * low_out + HIGH_PASS[0] * high_out + LOW_PASS[2] * low_prev + HIGH_PASS[2] * high_prev
    odd_part = LOW_PASS[1] * low_out + HIGH_PASS[1] * high_out + LOW_PASS[3] * low_prev + HIGH_PASS[3] * high_prev
    return jnp.stack([even_part, odd_part], axis=-1).reshape(PORTS, total)
```

```python
import functools
import math

import jax
import jax.numpy as jnp
import numpy as np
from jax import lax
from jax.experimental import pallas as pl
from jax.experimental.pallas import tpu as pltpu
from jax.sharding import Mesh, PartitionSpec as P

ROOT_THREE = math.sqrt(3.0)
SCALE_NORM = 4.0 * math.sqrt(2.0)
LOW_PASS = (
    (1.0 + ROOT_THREE) / SCALE_NORM,
    (3.0 + ROOT_THREE) / SCALE_NORM,
    (3.0 - ROOT_THREE) / SCALE_NORM,
    (1.0 - ROOT_THREE) / SCALE_NORM,
)
HIGH_PASS = (LOW_PASS[3], -LOW_PASS[2], LOW_PASS[1], -LOW_PASS[0])

NY, NZ, NC, NR = 4, 16, 2, 4
SEG = ("y", "z", "core")
PLANE = ("y", "core")
BS = 128
BLOCKS_HERE = 48
MARGIN = BLOCKS_HERE // 4
WINDOW = BLOCKS_HERE + 2 * MARGIN
BLOCKS_ALL = BLOCKS_HERE * NY * NZ * NC
LOWS = BLOCKS_HERE // 2
KEPT = BLOCKS_HERE // NR
PORTS_DEV = 8
PORTS = PORTS_DEV * NR
NNZ = 128
NNZ_STEP = 16
UP_ROWS = MARGIN + 2
VMEM = pl.BlockSpec(memory_space=pltpu.VMEM)
SMEM = pl.BlockSpec(memory_space=pltpu.SMEM)
PARAMS = pltpu.CompilerParams(vmem_limit_bytes=48 * 1024 * 1024)


def forward_matrix():
    taps = np.zeros((3 * BS, 2 * BS), np.float32)
    for k in range(BS):
        for j in range(4):
            taps[2 * k + j, k] = LOW_PASS[j]
            taps[2 * k + j, BS + k] = HIGH_PASS[j]
    return taps


def inverse_matrix():
    taps = np.zeros((4 * BS, 2 * BS), np.float32)
    for k in range(BS):
        for odd in range(2):
            taps[k, 2 * k + odd] = LOW_PASS[odd]
            taps[BS + k, 2 * k + odd] = HIGH_PASS[odd]
            before = k - 1 if k else 2 * BS + BS - 1
            taps[before, 2 * k + odd] = LOW_PASS[2 + odd]
            before = BS + k - 1 if k else 3 * BS + BS - 1
            taps[before, 2 * k + odd] = HIGH_PASS[2 + odd]
    return taps


def dot_exact(a, b):
    return jnp.dot(a, b, precision=lax.Precision.HIGHEST, preferred_element_type=jnp.float32)


def forward_kernel(x_ref, next_ref, taps_ref, out_ref):
    wide = 2 * BS
    here = jnp.concatenate(
        [x_ref[:, wide * b : wide * (b + 1)] for b in range(LOWS)], axis=0
    )
    after = jnp.concatenate(
        [x_ref[:, wide * b : wide * b + BS] for b in range(1, LOWS)] + [next_ref[...]], axis=0
    )
    bands = dot_exact(here, taps_ref[:wide]) + dot_exact(after, taps_ref[wide:])
    bands = bands.astype(jnp.bfloat16)
    for b in range(BLOCKS_HERE):
        rows = PORTS_DEV * (b % LOWS)
        lanes = BS * (b // LOWS)
        out_ref[b % NR, b // NR] = bands[rows : rows + PORTS_DEV, lanes : lanes + BS]


def select_kernel(wanted_ref, table_ref, out_ref):
    source = lax.axis_index("y") * (NZ * NC) + lax.axis_index("core")

    def one(step, carry):
        reader = step // NZ
        z = step % NZ
        for k in range(2):
            block = jnp.maximum(wanted_ref[reader, k, source + NC * z], 0) // NR
            for half in range(2):
                out_ref[reader, half, 2 * z + k] = table_ref[z, half, block]
        return carry

    lax.fori_loop(0, NY * NC * NZ, one, 0, unroll=8)


def product_kernel(
    rows_ref, slots_ref, first_ref, second_ref, coupling_ref, total_ref, up_ref, down_ref
):
    step = pl.program_id(0)
    seg = (lax.axis_index("y") * NZ + lax.axis_index("z")) * NC + lax.axis_index("core")
    edge = seg * BLOCKS_HERE - MARGIN

    @pl.when(step == 0)
    def _():
        total_ref[...] = jnp.zeros_like(total_ref)

    for i in range(NNZ_STEP):
        n = step * NNZ_STEP + i
        row = (rows_ref[0, n] - edge + BLOCKS_ALL) % BLOCKS_ALL
        slot = slots_ref[0, n]
        source = slot // 2
        group = source // (NZ * NC) * NC + source % NC
        place = (source // NC) % NZ * 2 + slot % 2
        vector = jnp.concatenate(
            [
                first_ref[group, 0, place],
                first_ref[group, 1, place],
                second_ref[group, 0, place],
                second_ref[group, 1, place],
            ],
            axis=0,
        )
        product = lax.dot_general(
            vector,
            coupling_ref[i],
            (((1,), (1,)), ((), ())),
            preferred_element_type=jnp.float32,
        )
        total_ref[row] += product

    @pl.when(step == NNZ // NNZ_STEP - 1)
    def _():
        down_ref[...] = total_ref[:MARGIN].astype(jnp.bfloat16)
        up_ref[:MARGIN] = total_ref[MARGIN + BLOCKS_HERE :].astype(jnp.bfloat16)
        up_ref[MARGIN] = total_ref[MARGIN + LOWS - 1].astype(jnp.bfloat16)
        up_ref[MARGIN + 1] = total_ref[MARGIN + BLOCKS_HERE - 1].astype(jnp.bfloat16)


def combine_kernel(total_ref, above_ref, below_ref, out_ref):
    for row in range(BLOCKS_HERE + 2):
        if row < BLOCKS_HERE:
            value = total_ref[MARGIN + row]
            if row < MARGIN:
                value = value + above_ref[row].astype(jnp.float32)
            if row >= BLOCKS_HERE - MARGIN:
                value = value + below_ref[row - BLOCKS_HERE + MARGIN].astype(jnp.float32)
        else:
            value = above_ref[MARGIN + row - BLOCKS_HERE].astype(jnp.float32)
            if row == BLOCKS_HERE + 1:
                value = value + total_ref[MARGIN - 1]
        for r in range(NR):
            out_ref[r, row] = value[PORTS_DEV * r : PORTS_DEV * (r + 1)].astype(jnp.bfloat16)


def inverse_kernel(parts_ref, taps_ref, out_ref):
    rows = parts_ref[0].astype(jnp.float32)
    for r in range(1, NR):
        rows = rows + parts_ref[r].astype(jnp.float32)
    flat = LOWS * PORTS_DEV
    low = rows[:LOWS].reshape(flat, BS)
    high = rows[LOWS:BLOCKS_HERE].reshape(flat, BS)
    low_before = jnp.concatenate([rows[BLOCKS_HERE], low[: flat - PORTS_DEV]], axis=0)
    high_before = jnp.concatenate([rows[BLOCKS_HERE + 1], high[: flat - PORTS_DEV]], axis=0)
    stacked = jnp.concatenate([low, high, low_before, high_before], axis=1)
    volts = dot_exact(stacked, taps_ref[...])
    for b in range(LOWS):
        out_ref[:, 2 * BS * b : 2 * BS * (b + 1)] = volts[PORTS_DEV * b : PORTS_DEV * (b + 1)]


def shift(block, distance):
    count = NY * NZ * NC
    route = [(i, (i + distance) % count) for i in range(count)]
    return lax.ppermute(block, SEG, route)


def shards(currents, requested, block_rows, block_slots, coupling):
    bf16 = jnp.bfloat16
    next_head = shift(currents[:, :BS], -1)
    wanted = lax.all_gather(requested[0, 0].T, PLANE, axis=0)
    residues = pl.pallas_call(
        forward_kernel,
        out_shape=jax.ShapeDtypeStruct((NR, KEPT, PORTS_DEV, BS), bf16),
        in_specs=[VMEM, VMEM, VMEM],
        out_specs=VMEM,
        compiler_params=PARAMS,
        name="forward",
    )(currents, next_head, jnp.asarray(forward_matrix()))
    residues = lax.all_to_all(residues, "rep", 0, 0, tiled=True)

    def fetch(part):
        table = lax.all_gather(part, "z", axis=0)
        chosen = pl.pallas_call(
            select_kernel,
            out_shape=jax.ShapeDtypeStruct((NY * NC, 2, 2 * NZ, PORTS_DEV, BS), bf16),
            in_specs=[SMEM, VMEM],
            out_specs=VMEM,
            compiler_params=PARAMS,
            name="select",
        )(wanted, table)
        return lax.all_to_all(chosen, PLANE, 0, 0, tiled=True)

    first = fetch(residues[:2])
    second = fetch(residues[2:])
    whole = lambda *shape: pl.BlockSpec(shape, lambda n: (0,) * len(shape))
    total, up, down = pl.pallas_call(
        product_kernel,
        grid=(NNZ // NNZ_STEP,),
        out_shape=[
            jax.ShapeDtypeStruct((WINDOW, PORTS, BS), jnp.float32),
            jax.ShapeDtypeStruct((UP_ROWS, PORTS, BS), bf16),
            jax.ShapeDtypeStruct((MARGIN, PORTS, BS), bf16),
        ],
        in_specs=[
            SMEM,
            SMEM,
            whole(*first.shape),
            whole(*second.shape),
            pl.BlockSpec((NNZ_STEP, BS, BS), lambda n: (n, 0, 0)),
        ],
        out_specs=[
            whole(WINDOW, PORTS, BS),
            whole(UP_ROWS, PORTS, BS),
            whole(MARGIN, PORTS, BS),
        ],
        compiler_params=PARAMS,
        name="products",
    )(block_rows[0], block_slots[0], first, second, coupling[0, 0])
    above = shift(up, 1)
    below = shift(down, -1)
    parts = pl.pallas_call(
        combine_kernel,
        out_shape=jax.ShapeDtypeStruct((NR, BLOCKS_HERE + 2, PORTS_DEV, BS), bf16),
        in_specs=[VMEM, VMEM, VMEM],
        out_specs=VMEM,
        compiler_params=PARAMS,
        name="combine",
    )(total, above, below)
    parts = lax.all_to_all(parts, "rep", 0, 0, tiled=True)
    return pl.pallas_call(
        inverse_kernel,
        out_shape=jax.ShapeDtypeStruct(currents.shape, jnp.float32),
        in_specs=[VMEM, VMEM],
        out_specs=VMEM,
        compiler_params=PARAMS,
        name="inverse",
    )(parts, jnp.asarray(inverse_matrix()))


def solution(mesh):
    grid = Mesh(mesh.devices.reshape(NY, NZ, NC, NR), SEG + ("rep",))
    placed = (
        P("rep", SEG),
        P(SEG, "rep", None, None),
        P(SEG, "rep", None),
        P(SEG, "rep", None),
        P(SEG, "rep", None, None, None),
    )
    return jax.shard_map(
        shards, mesh=grid, in_specs=placed, out_specs=P("rep", SEG), check_vma=False
    )
```

```python
import math

import jax
import jax.numpy as jnp
import numpy as np
from jax import lax
from jax.experimental import pallas as pl
from jax.experimental.pallas import tpu as pltpu
from jax.sharding import Mesh, PartitionSpec as P

ROOT_THREE = math.sqrt(3.0)
SCALE_NORM = 4.0 * math.sqrt(2.0)
LOW_PASS = (
    (1.0 + ROOT_THREE) / SCALE_NORM,
    (3.0 + ROOT_THREE) / SCALE_NORM,
    (3.0 - ROOT_THREE) / SCALE_NORM,
    (1.0 - ROOT_THREE) / SCALE_NORM,
)
HIGH_PASS = (LOW_PASS[3], -LOW_PASS[2], LOW_PASS[1], -LOW_PASS[0])

NY, NZ, NC, NR = 4, 16, 2, 4
FINE = ("y", "zhigh", "zlow", "core")
EVERY = FINE + ("rep",)
NH = 4
NL = NZ // NH
BS = 128
BLOCKS_HERE = 48
MARGIN = BLOCKS_HERE // 4
WINDOW = BLOCKS_HERE + 2 * MARGIN
BLOCKS_ALL = BLOCKS_HERE * NY * NZ * NC
LOWS = BLOCKS_HERE // 2
SLOTS = NH * NC * 2
PORTS_DEV = 8
PORTS = PORTS_DEV * NR
NNZ = 128
NNZ_STEP = 16
UP_ROWS = MARGIN + 2
VMEM = pl.BlockSpec(memory_space=pltpu.VMEM)
SMEM = pl.BlockSpec(memory_space=pltpu.SMEM)
PARAMS = pltpu.CompilerParams(vmem_limit_bytes=48 * 1024 * 1024)


def forward_matrix():
    taps = np.zeros((3 * BS, 2 * BS), np.float32)
    for k in range(BS):
        for j in range(4):
            taps[2 * k + j, k] = LOW_PASS[j]
            taps[2 * k + j, BS + k] = HIGH_PASS[j]
    return taps


def inverse_matrix():
    taps = np.zeros((4 * BS, 2 * BS), np.float32)
    for k in range(BS):
        for odd in range(2):
            taps[k, 2 * k + odd] = LOW_PASS[odd]
            taps[BS + k, 2 * k + odd] = HIGH_PASS[odd]
            before = k - 1 if k else 2 * BS + BS - 1
            taps[before, 2 * k + odd] = LOW_PASS[2 + odd]
            before = BS + k - 1 if k else 3 * BS + BS - 1
            taps[before, 2 * k + odd] = HIGH_PASS[2 + odd]
    return taps


def dot_exact(a, b):
    return jnp.dot(a, b, precision=lax.Precision.HIGHEST, preferred_element_type=jnp.float32)


def forward_kernel(x_ref, next_ref, taps_ref, out_ref):
    wide = 2 * BS
    here = jnp.concatenate(
        [x_ref[:, wide * b : wide * (b + 1)] for b in range(LOWS)], axis=0
    )
    after = jnp.concatenate(
        [x_ref[:, wide * b : wide * b + BS] for b in range(1, LOWS)] + [next_ref[...]], axis=0
    )
    bands = dot_exact(here, taps_ref[:wide]) + dot_exact(after, taps_ref[wide:])
    bands = bands.astype(jnp.bfloat16)
    for b in range(BLOCKS_HERE):
        rows = PORTS_DEV * (b % LOWS)
        lanes = BS * (b // LOWS)
        out_ref[b] = bands[rows : rows + PORTS_DEV, lanes : lanes + BS]


def select_kernel(wanted_ref, table_ref, out_ref):
    def one(reader, carry):
        for high in range(NH):
            for core in range(NC):
                for k in range(2):
                    slot = (high * NC + core) * 2 + k
                    block = jnp.maximum(wanted_ref[reader, slot], 0)
                    out_ref[reader, slot] = table_ref[core, high, block]
        return carry

    lax.fori_loop(0, NY * NL * NR, one, 0, unroll=2)


def seg_index():
    high = lax.axis_index("y") * NH + lax.axis_index("zhigh")
    return (high * NL + lax.axis_index("zlow")) * NC + lax.axis_index("core")


def product_kernel(rows_ref, slots_ref, vectors_ref, coupling_ref, total_ref, near_ref, far_ref):
    step = pl.program_id(0)
    edge = seg_index() * BLOCKS_HERE - MARGIN

    @pl.when(step == 0)
    def _():
        total_ref[...] = jnp.zeros_like(total_ref)

    for i in range(NNZ_STEP):
        n = step * NNZ_STEP + i
        row = rows_ref[0, n] - edge
        row = jnp.where(row < 0, row + BLOCKS_ALL, row)
        row = jnp.where(row >= BLOCKS_ALL, row - BLOCKS_ALL, row)
        slot = slots_ref[0, n]
        source = slot >> 1
        z = (source >> 1) & (NZ - 1)
        sender = (source >> 5) * NL + (z & (NL - 1))
        place = ((z >> 2) * NC + (source & 1)) * 2 + (slot & 1)
        vector = jnp.concatenate([vectors_ref[sender, r, place] for r in range(NR)], axis=0)
        product = lax.dot_general(
            vector,
            coupling_ref[i],
            (((1,), (1,)), ((), ())),
            preferred_element_type=jnp.float32,
        )
        total_ref[row] += product

    def margins(up_ref, down_ref):
        down_ref[:MARGIN] = total_ref[:MARGIN].astype(jnp.bfloat16)
        down_ref[MARGIN:] = jnp.zeros((2, PORTS, BS), jnp.bfloat16)
        up_ref[:MARGIN] = total_ref[MARGIN + BLOCKS_HERE :].astype(jnp.bfloat16)
        up_ref[MARGIN] = total_ref[MARGIN + LOWS - 1].astype(jnp.bfloat16)
        up_ref[MARGIN + 1] = total_ref[MARGIN + BLOCKS_HERE - 1].astype(jnp.bfloat16)

    last = step == NNZ // NNZ_STEP - 1
    core = lax.axis_index("core")
    pl.when(last & (core == 0))(lambda: margins(near_ref, far_ref))
    pl.when(last & (core == 1))(lambda: margins(far_ref, near_ref))


def combine_kernel(total_ref, near_ref, far_ref, out_ref):
    def combine(above_ref, below_ref):
        for row in range(BLOCKS_HERE + 2):
            if row < BLOCKS_HERE:
                value = total_ref[MARGIN + row]
                if row < MARGIN:
                    value = value + above_ref[row].astype(jnp.float32)
                if row >= BLOCKS_HERE - MARGIN:
                    value = value + below_ref[row - BLOCKS_HERE + MARGIN].astype(jnp.float32)
            else:
                value = above_ref[MARGIN + row - BLOCKS_HERE].astype(jnp.float32)
                if row == BLOCKS_HERE + 1:
                    value = value + total_ref[MARGIN - 1]
            for r in range(NR):
                out_ref[r, row] = value[PORTS_DEV * r : PORTS_DEV * (r + 1)].astype(jnp.bfloat16)

    core = lax.axis_index("core")
    pl.when(core == 0)(lambda: combine(far_ref, near_ref))
    pl.when(core == 1)(lambda: combine(near_ref, far_ref))


def inverse_kernel(parts_ref, taps_ref, out_ref):
    rows = parts_ref[0].astype(jnp.float32)
    for r in range(1, NR):
        rows = rows + parts_ref[r].astype(jnp.float32)
    flat = LOWS * PORTS_DEV
    low = rows[:LOWS].reshape(flat, BS)
    high = rows[LOWS:BLOCKS_HERE].reshape(flat, BS)
    low_before = jnp.concatenate([rows[BLOCKS_HERE], low[: flat - PORTS_DEV]], axis=0)
    high_before = jnp.concatenate([rows[BLOCKS_HERE + 1], high[: flat - PORTS_DEV]], axis=0)
    stacked = jnp.concatenate([low, high, low_before, high_before], axis=1)
    volts = dot_exact(stacked, taps_ref[...])
    for b in range(LOWS):
        out_ref[:, 2 * BS * b : 2 * BS * (b + 1)] = volts[PORTS_DEV * b : PORTS_DEV * (b + 1)]


def route(block, partner):
    count = NY * NZ * NC
    return lax.ppermute(block, FINE, [(i, partner(i) % count) for i in range(count)])


def windows():
    groups = []
    for core in range(NC):
        for high in range(NH):
            start = NL * high + 2 * core
            members = sorted((z % NL, z % NZ) for z in range(start, start + NL))
            groups.append(
                [
                    ((y * NZ + z) * NC + core) * NR + r
                    for y in range(NY)
                    for _, z in members
                    for r in range(NR)
                ]
            )
    return groups


def to_window(block):
    return lax.all_to_all(block, EVERY, 0, 0, tiled=True, axis_index_groups=windows())


def shards(currents, requested, block_rows, block_slots, coupling):
    bf16 = jnp.bfloat16
    next_head = route(currents[:, :BS], lambda i: i - 1)
    wanted = requested.reshape(NY, NH, NL, NC, 2).transpose(0, 2, 1, 3, 4)
    wanted = jnp.broadcast_to(wanted.reshape(NY, NL, 1, SLOTS), (NY, NL, NR, SLOTS))
    wanted = to_window(wanted.reshape(NY * NL * NR, SLOTS))
    table = pl.pallas_call(
        forward_kernel,
        out_shape=jax.ShapeDtypeStruct((BLOCKS_HERE, PORTS_DEV, BS), bf16),
        in_specs=[VMEM, VMEM, VMEM],
        out_specs=VMEM,
        compiler_params=PARAMS,
        name="forward",
    )(currents, next_head, jnp.asarray(forward_matrix()))
    table = lax.all_gather(table, "zhigh", axis=0)
    table = lax.all_gather(table, "core", axis=0)
    chosen = pl.pallas_call(
        select_kernel,
        out_shape=jax.ShapeDtypeStruct((NY * NL * NR, SLOTS, PORTS_DEV, BS), bf16),
        in_specs=[SMEM, VMEM],
        out_specs=VMEM,
        compiler_params=PARAMS,
        name="select",
    )(wanted, table)
    vectors = to_window(chosen).reshape(NY * NL, NR, SLOTS, PORTS_DEV, BS)
    whole = lambda *shape: pl.BlockSpec(shape, lambda n: (0,) * len(shape))
    total, near, far = pl.pallas_call(
        product_kernel,
        grid=(NNZ // NNZ_STEP,),
        out_shape=[
            jax.ShapeDtypeStruct((WINDOW, PORTS, BS), jnp.float32),
            jax.ShapeDtypeStruct((UP_ROWS, PORTS, BS), bf16),
            jax.ShapeDtypeStruct((UP_ROWS, PORTS, BS), bf16),
        ],
        in_specs=[
            SMEM,
            SMEM,
            whole(*vectors.shape),
            pl.BlockSpec((NNZ_STEP, BS, BS), lambda n: (n, 0, 0)),
        ],
        out_specs=[
            whole(WINDOW, PORTS, BS),
            whole(UP_ROWS, PORTS, BS),
            whole(UP_ROWS, PORTS, BS),
        ],
        compiler_params=PARAMS,
        name="products",
    )(block_rows[0], block_slots[0], vectors, coupling[0, 0])
    near = route(near, lambda i: i ^ 1)
    far = route(far, lambda i: i + 1 if i % 2 else i - 1)
    parts = pl.pallas_call(
        combine_kernel,
        out_shape=jax.ShapeDtypeStruct((NR, BLOCKS_HERE + 2, PORTS_DEV, BS), bf16),
        in_specs=[VMEM, VMEM, VMEM],
        out_specs=VMEM,
        compiler_params=PARAMS,
        name="combine",
    )(total, near, far)
    parts = lax.all_to_all(parts, "rep", 0, 0, tiled=True)
    return pl.pallas_call(
        inverse_kernel,
        out_shape=jax.ShapeDtypeStruct(currents.shape, jnp.float32),
        in_specs=[VMEM, VMEM],
        out_specs=VMEM,
        compiler_params=PARAMS,
        name="inverse",
    )(parts, jnp.asarray(inverse_matrix()))


def solution(mesh):
    grid = Mesh(mesh.devices.reshape(NY, NH, NL, NC, NR), EVERY)
    placed = (
        P("rep", FINE),
        P(FINE, "rep", None, None),
        P(FINE, "rep", None),
        P(FINE, "rep", None),
        P(FINE, "rep", None, None, None),
    )
    return jax.shard_map(
        shards, mesh=grid, in_specs=placed, out_specs=P("rep", FINE), check_vma=False
    )
```

```python
import math

import jax
import jax.numpy as jnp
import numpy as np
from jax import lax
from jax.experimental import pallas as pl
from jax.experimental.pallas import tpu as pltpu
from jax.sharding import Mesh, PartitionSpec as P

ROOT_THREE = math.sqrt(3.0)
SCALE_NORM = 4.0 * math.sqrt(2.0)
LOW_PASS = (
    (1.0 + ROOT_THREE) / SCALE_NORM,
    (3.0 + ROOT_THREE) / SCALE_NORM,
    (3.0 - ROOT_THREE) / SCALE_NORM,
    (1.0 - ROOT_THREE) / SCALE_NORM,
)
HIGH_PASS = (LOW_PASS[3], -LOW_PASS[2], LOW_PASS[1], -LOW_PASS[0])

NY, NZ, NC, NR = 4, 16, 2, 4
FINE = ("y", "zhigh", "zmid", "zlow", "core")
EVERY = FINE + ("rep",)
NH, NM, NL = 4, 2, 2
BS = 128
BLOCKS_HERE = 48
MARGIN = BLOCKS_HERE // 4
WINDOW = BLOCKS_HERE + 2 * MARGIN
BLOCKS_ALL = BLOCKS_HERE * NY * NZ * NC
LOWS = BLOCKS_HERE // 2
SLOTS = NH * NL * NC * 2
PORTS_DEV = 8
PORTS = PORTS_DEV * NR
NNZ = 128
NNZ_STEP = 16
UP_ROWS = MARGIN + 2
VMEM = pl.BlockSpec(memory_space=pltpu.VMEM)
SMEM = pl.BlockSpec(memory_space=pltpu.SMEM)
PARAMS = pltpu.CompilerParams(vmem_limit_bytes=48 * 1024 * 1024)


def inverse_matrix():
    taps = np.zeros((4 * BS, 2 * BS), np.float32)
    for k in range(BS):
        for odd in range(2):
            taps[k, 2 * k + odd] = LOW_PASS[odd]
            taps[BS + k, 2 * k + odd] = HIGH_PASS[odd]
            before = k - 1 if k else 2 * BS + BS - 1
            taps[before, 2 * k + odd] = LOW_PASS[2 + odd]
            before = BS + k - 1 if k else 3 * BS + BS - 1
            taps[before, 2 * k + odd] = HIGH_PASS[2 + odd]
    return taps


def dot_exact(a, b):
    return jnp.dot(a, b, precision=lax.Precision.HIGHEST, preferred_element_type=jnp.float32)


def forward_kernel(x_ref, next_ref, out_ref):
    wide = 2 * BS
    row = lax.broadcasted_iota(jnp.int32, (wide + BS, wide), 0)
    lane = lax.broadcasted_iota(jnp.int32, (wide + BS, wide), 1)
    is_low = lane < BS
    tap = row - 2 * jnp.where(is_low, lane, lane - BS)
    taps = jnp.zeros((wide + BS, wide), jnp.float32)
    for j in range(4):
        taps = jnp.where(tap == j, jnp.where(is_low, LOW_PASS[j], HIGH_PASS[j]), taps)
    here = jnp.concatenate(
        [x_ref[:, wide * b : wide * (b + 1)] for b in range(LOWS)], axis=0
    )
    after = jnp.concatenate(
        [x_ref[:, wide * b : wide * b + BS] for b in range(1, LOWS)] + [next_ref[...]], axis=0
    )
    bands = dot_exact(here, taps[:wide]) + dot_exact(after, taps[wide:])
    bands = bands.astype(jnp.bfloat16)
    for b in range(BLOCKS_HERE):
        rows = PORTS_DEV * (b % LOWS)
        lanes = BS * (b // LOWS)
        out_ref[b] = bands[rows : rows + PORTS_DEV, lanes : lanes + BS]


def select_kernel(wanted_ref, same_ref, other_ref, out_ref):
    parity = lax.axis_index("zlow")

    def one(reader, carry):
        for high in range(NH):
            for swap, table_ref in enumerate((same_ref, other_ref)):
                asked = (high * NL + (parity ^ swap)) * NC * 2
                given = (high * NL + swap) * NC * 2
                for core in range(NC):
                    for k in range(2):
                        block = jnp.maximum(wanted_ref[reader, asked + 2 * core + k], 0)
                        out_ref[reader, given + 2 * core + k] = table_ref[core, high, block]
        return carry

    lax.fori_loop(0, NY * NM * NR, one, 0)


def seg_index():
    z = lax.axis_index("zhigh") * NM + lax.axis_index("zmid")
    z = z * NL + lax.axis_index("zlow")
    return (lax.axis_index("y") * NZ + z) * NC + lax.axis_index("core")


def product_kernel(rows_ref, slots_ref, vectors_ref, coupling_ref, total_ref, near_ref, far_ref):
    step = pl.program_id(0)
    edge = seg_index() * BLOCKS_HERE - MARGIN
    parity = lax.axis_index("zlow")

    @pl.when(step == 0)
    def _():
        total_ref[...] = jnp.zeros_like(total_ref)

    for i in range(NNZ_STEP):
        n = step * NNZ_STEP + i
        row = rows_ref[0, n] - edge
        row = jnp.where(row < 0, row + BLOCKS_ALL, row)
        row = jnp.where(row >= BLOCKS_ALL, row - BLOCKS_ALL, row)
        slot = slots_ref[0, n]
        source = slot >> 1
        z = (source >> 1) & (NZ - 1)
        sender = (source >> 5) * NM + ((z >> 1) & 1)
        place = ((z >> 2) * NL + ((z & 1) ^ parity)) * NC * 2 + (slot & 3)
        vector = jnp.concatenate([vectors_ref[sender, r, place] for r in range(NR)], axis=0)
        product = lax.dot_general(
            vector,
            coupling_ref[i],
            (((1,), (1,)), ((), ())),
            preferred_element_type=jnp.float32,
        )
        total_ref[row] += product

    def margins(up_ref, down_ref):
        down_ref[:MARGIN] = total_ref[:MARGIN].astype(jnp.bfloat16)
        down_ref[MARGIN:] = jnp.zeros((2, PORTS, BS), jnp.bfloat16)
        up_ref[:MARGIN] = total_ref[MARGIN + BLOCKS_HERE :].astype(jnp.bfloat16)
        up_ref[MARGIN] = total_ref[MARGIN + LOWS - 1].astype(jnp.bfloat16)
        up_ref[MARGIN + 1] = total_ref[MARGIN + BLOCKS_HERE - 1].astype(jnp.bfloat16)

    last = step == NNZ // NNZ_STEP - 1
    core = lax.axis_index("core")
    pl.when(last & (core == 0))(lambda: margins(near_ref, far_ref))
    pl.when(last & (core == 1))(lambda: margins(far_ref, near_ref))


def combine_kernel(total_ref, nears_ref, far_ref, out_ref):
    def combine(above_ref, below_ref):
        for row in range(BLOCKS_HERE + 2):
            if row < BLOCKS_HERE:
                value = total_ref[MARGIN + row]
                if row < MARGIN:
                    value = value + above_ref[row].astype(jnp.float32)
                if row >= BLOCKS_HERE - MARGIN:
                    value = value + below_ref[row - BLOCKS_HERE + MARGIN].astype(jnp.float32)
            else:
                value = above_ref[MARGIN + row - BLOCKS_HERE].astype(jnp.float32)
                if row == BLOCKS_HERE + 1:
                    value = value + total_ref[MARGIN - 1]
            for r in range(NR):
                out_ref[r, row] = value[PORTS_DEV * r : PORTS_DEV * (r + 1)].astype(jnp.bfloat16)

    core = lax.axis_index("core")
    pl.when(core == 0)(lambda: combine(far_ref, nears_ref.at[1]))
    pl.when(core == 1)(lambda: combine(nears_ref.at[0], far_ref))


def inverse_kernel(parts_ref, taps_ref, out_ref):
    rows = parts_ref[0].astype(jnp.float32)
    for r in range(1, NR):
        rows = rows + parts_ref[r].astype(jnp.float32)
    flat = LOWS * PORTS_DEV
    low = rows[:LOWS].reshape(flat, BS)
    high = rows[LOWS:BLOCKS_HERE].reshape(flat, BS)
    low_before = jnp.concatenate([rows[BLOCKS_HERE], low[: flat - PORTS_DEV]], axis=0)
    high_before = jnp.concatenate([rows[BLOCKS_HERE + 1], high[: flat - PORTS_DEV]], axis=0)
    stacked = jnp.concatenate([low, high, low_before, high_before], axis=1)
    volts = dot_exact(stacked, taps_ref[...])
    for b in range(LOWS):
        out_ref[:, 2 * BS * b : 2 * BS * (b + 1)] = volts[PORTS_DEV * b : PORTS_DEV * (b + 1)]


def route(block, partner):
    count = NY * NZ * NC
    return lax.ppermute(block, FINE, [(i, partner(i) % count) for i in range(count)])


def windows():
    groups = []
    for core in range(NC):
        for first in range(0, NZ, 4):
            for odd in range(2):
                start = first + odd + 2 * core
                members = sorted(((z >> 1) & 1, z % NZ) for z in (start, start + 2))
                groups.append(
                    [
                        ((y * NZ + z) * NC + core) * NR + r
                        for y in range(NY)
                        for _, z in members
                        for r in range(NR)
                    ]
                )
    return groups


def to_window(block):
    return lax.all_to_all(block, EVERY, 0, 0, tiled=True, axis_index_groups=windows())


def shards(currents, requested, block_rows, block_slots, coupling):
    bf16 = jnp.bfloat16
    next_head = route(currents[:, :BS], lambda i: i - 1)
    same = pl.pallas_call(
        forward_kernel,
        out_shape=jax.ShapeDtypeStruct((BLOCKS_HERE, PORTS_DEV, BS), bf16),
        in_specs=[VMEM, VMEM],
        out_specs=VMEM,
        compiler_params=PARAMS,
        name="forward",
    )(currents, next_head)
    wanted = requested.reshape(NY, NH, NM, NL * NC * 2).transpose(0, 2, 1, 3)
    wanted = jnp.broadcast_to(wanted.reshape(NY, NM, 1, SLOTS), (NY, NM, NR, SLOTS))
    wanted = wanted.reshape(NY * NM * NR, SLOTS)
    same = lax.all_gather(same, "zhigh", axis=0)
    same, wanted = lax.optimization_barrier((same, wanted))
    other = route(same, lambda i: i ^ NC)
    same = lax.all_gather(same, "core", axis=0)
    wanted = to_window(wanted)
    other = lax.all_gather(other, "core", axis=0)
    chosen = pl.pallas_call(
        select_kernel,
        out_shape=jax.ShapeDtypeStruct((NY * NM * NR, SLOTS, PORTS_DEV, BS), bf16),
        in_specs=[SMEM, VMEM, VMEM],
        out_specs=VMEM,
        compiler_params=PARAMS,
        name="select",
    )(wanted, same, other)
    vectors = to_window(chosen).reshape(NY * NM, NR, SLOTS, PORTS_DEV, BS)
    whole = lambda *shape: pl.BlockSpec(shape, lambda n: (0,) * len(shape))
    total, near, far = pl.pallas_call(
        product_kernel,
        grid=(NNZ // NNZ_STEP,),
        out_shape=[
            jax.ShapeDtypeStruct((WINDOW, PORTS, BS), jnp.float32),
            jax.ShapeDtypeStruct((UP_ROWS, PORTS, BS), bf16),
            jax.ShapeDtypeStruct((UP_ROWS, PORTS, BS), bf16),
        ],
        in_specs=[
            SMEM,
            SMEM,
            whole(*vectors.shape),
            pl.BlockSpec((NNZ_STEP, BS, BS), lambda n: (n, 0, 0)),
        ],
        out_specs=[
            whole(WINDOW, PORTS, BS),
            whole(UP_ROWS, PORTS, BS),
            whole(UP_ROWS, PORTS, BS),
        ],
        compiler_params=PARAMS,
        name="products",
    )(block_rows[0], block_slots[0], vectors, coupling[0, 0])
    nears = lax.all_gather(near, "core", axis=0)
    far = route(far, lambda i: i + 1 if i % 2 else i - 1)
    parts = pl.pallas_call(
        combine_kernel,
        out_shape=jax.ShapeDtypeStruct((NR, BLOCKS_HERE + 2, PORTS_DEV, BS), bf16),
        in_specs=[VMEM, VMEM, VMEM],
        out_specs=VMEM,
        compiler_params=PARAMS,
        name="combine",
    )(total, nears, far)
    parts = lax.all_to_all(parts, "rep", 0, 0, tiled=True)
    return pl.pallas_call(
        inverse_kernel,
        out_shape=jax.ShapeDtypeStruct(currents.shape, jnp.float32),
        in_specs=[VMEM, VMEM],
        out_specs=VMEM,
        compiler_params=PARAMS,
        name="inverse",
    )(parts, jnp.asarray(inverse_matrix()))


def solution(mesh):
    grid = Mesh(mesh.devices.reshape(NY, NH, NM, NL, NC, NR), EVERY)
    placed = (
        P("rep", FINE),
        P(FINE, "rep", None, None),
        P(FINE, "rep", None),
        P(FINE, "rep", None),
        P(FINE, "rep", None, None, None),
    )
    return jax.shard_map(
        shards, mesh=grid, in_specs=placed, out_specs=P("rep", FINE), check_vma=False
    )
```

```python
import math

import jax
import jax.numpy as jnp
import numpy as np
from jax import lax
from jax.experimental import pallas as pl
from jax.experimental.pallas import tpu as pltpu
from jax.sharding import Mesh, PartitionSpec as P

ROOT_THREE = math.sqrt(3.0)
SCALE_NORM = 4.0 * math.sqrt(2.0)
LOW_PASS = (
    (1.0 + ROOT_THREE) / SCALE_NORM,
    (3.0 + ROOT_THREE) / SCALE_NORM,
    (3.0 - ROOT_THREE) / SCALE_NORM,
    (1.0 - ROOT_THREE) / SCALE_NORM,
)
HIGH_PASS = (LOW_PASS[3], -LOW_PASS[2], LOW_PASS[1], -LOW_PASS[0])

NY, NZ, NC, NR = 4, 16, 2, 4
FINE = ("y", "zhigh", "zmid", "zlow", "core")
EVERY = FINE + ("rep",)
NH, NM, NL = 4, 2, 2
BS = 128
BLOCKS_HERE = 48
MARGIN = BLOCKS_HERE // 4
WINDOW = BLOCKS_HERE + 2 * MARGIN
KEPT = BLOCKS_HERE // NR
BLOCKS_ALL = BLOCKS_HERE * NY * NZ * NC
LOWS = BLOCKS_HERE // 2
SLOTS = NH * NL * NC * 2
PORTS_DEV = 8
PORTS = PORTS_DEV * NR
NNZ = 128
NNZ_STEP = 64
UP_ROWS = MARGIN + 2
VMEM = pl.BlockSpec(memory_space=pltpu.VMEM)
SMEM = pl.BlockSpec(memory_space=pltpu.SMEM)
PARAMS = pltpu.CompilerParams(vmem_limit_bytes=48 * 1024 * 1024)


def inverse_matrix():
    taps = np.zeros((4 * BS, 2 * BS), np.float32)
    for k in range(BS):
        for odd in range(2):
            taps[k, 2 * k + odd] = LOW_PASS[odd]
            taps[BS + k, 2 * k + odd] = HIGH_PASS[odd]
            before = k - 1 if k else 2 * BS + BS - 1
            taps[before, 2 * k + odd] = LOW_PASS[2 + odd]
            before = BS + k - 1 if k else 3 * BS + BS - 1
            taps[before, 2 * k + odd] = HIGH_PASS[2 + odd]
    return taps


def dot_exact(a, b):
    return jnp.dot(a, b, precision=lax.Precision.HIGHEST, preferred_element_type=jnp.float32)


def forward_kernel(x_ref, next_ref, out_ref):
    wide = 2 * BS
    row = lax.broadcasted_iota(jnp.int32, (wide + BS, wide), 0)
    lane = lax.broadcasted_iota(jnp.int32, (wide + BS, wide), 1)
    is_low = lane < BS
    tap = row - 2 * jnp.where(is_low, lane, lane - BS)
    taps = jnp.zeros((wide + BS, wide), jnp.float32)
    for j in range(4):
        taps = jnp.where(tap == j, jnp.where(is_low, LOW_PASS[j], HIGH_PASS[j]), taps)
    here = jnp.concatenate(
        [x_ref[:, wide * b : wide * (b + 1)] for b in range(LOWS)], axis=0
    )
    after = jnp.concatenate(
        [x_ref[:, wide * b : wide * b + BS] for b in range(1, LOWS)] + [next_ref[...]], axis=0
    )
    bands = dot_exact(here, taps[:wide]) + dot_exact(after, taps[wide:])
    bands = bands.astype(jnp.bfloat16)
    for b in range(BLOCKS_HERE):
        rows = PORTS_DEV * (b % LOWS)
        lanes = BS * (b // LOWS)
        out_ref[b % NR, b // NR] = bands[rows : rows + PORTS_DEV, lanes : lanes + BS]


def select_kernel(wanted_ref, same_ref, other_ref, out_ref):
    parity = lax.axis_index("zlow")

    def one(reader, carry):
        for high in range(NH):
            found = []
            for swap, table_ref in enumerate((same_ref, other_ref)):
                asked = (high * NL + (parity ^ swap)) * NC * 2
                for core in range(NC):
                    for k in range(2):
                        block = jnp.maximum(wanted_ref[reader, asked + 2 * core + k], 0)
                        found.append(table_ref[core, high, block >> 2])
            for i, block in enumerate(found):
                out_ref[reader, high * NL * NC * 2 + i] = block
        return carry

    lax.fori_loop(0, NY * NM, one, 0)


def seg_index():
    z = lax.axis_index("zhigh") * NM + lax.axis_index("zmid")
    z = z * NL + lax.axis_index("zlow")
    return (lax.axis_index("y") * NZ + z) * NC + lax.axis_index("core")


def product_kernel(rows_ref, slots_ref, vectors_ref, coupling_ref, total_ref, near_ref, far_ref):
    step = pl.program_id(0)
    edge = seg_index() * BLOCKS_HERE - MARGIN
    parity = lax.axis_index("zlow")

    @pl.when(step == 0)
    def _():
        total_ref[...] = jnp.zeros_like(total_ref)

    for i in range(NNZ_STEP):
        n = step * NNZ_STEP + i
        row = rows_ref[0, n] - edge
        row = jnp.where(row < 0, row + BLOCKS_ALL, row)
        row = jnp.where(row >= BLOCKS_ALL, row - BLOCKS_ALL, row)
        slot = slots_ref[0, n]
        source = slot >> 1
        z = (source >> 1) & (NZ - 1)
        sender = (source >> 5) * NM + ((z >> 1) & 1)
        place = ((z >> 2) * NL + ((z & 1) ^ parity)) * NC * 2 + (slot & 3)
        product = lax.dot_general(
            vectors_ref[sender, place],
            coupling_ref[i],
            (((1,), (1,)), ((), ())),
            preferred_element_type=jnp.float32,
        )
        total_ref[row] += product

    def margins(up_ref, down_ref):
        down_ref[:MARGIN] = total_ref[:MARGIN].astype(jnp.bfloat16)
        down_ref[MARGIN:] = jnp.zeros((2, PORTS, BS), jnp.bfloat16)
        up_ref[:MARGIN] = total_ref[MARGIN + BLOCKS_HERE :].astype(jnp.bfloat16)
        up_ref[MARGIN] = total_ref[MARGIN + LOWS - 1].astype(jnp.bfloat16)
        up_ref[MARGIN + 1] = total_ref[MARGIN + BLOCKS_HERE - 1].astype(jnp.bfloat16)

    last = step == NNZ // NNZ_STEP - 1
    core = lax.axis_index("core")
    pl.when(last & (core == 0))(lambda: margins(near_ref, far_ref))
    pl.when(last & (core == 1))(lambda: margins(far_ref, near_ref))


def combine_kernel(total_ref, nears_ref, far_ref, out_ref):
    def combine(above_ref, below_ref):
        for row in range(BLOCKS_HERE + 2):
            if row < BLOCKS_HERE:
                value = total_ref[MARGIN + row]
                if row < MARGIN:
                    value = value + above_ref[row].astype(jnp.float32)
                if row >= BLOCKS_HERE - MARGIN:
                    value = value + below_ref[row - BLOCKS_HERE + MARGIN].astype(jnp.float32)
            else:
                value = above_ref[MARGIN + row - BLOCKS_HERE].astype(jnp.float32)
                if row == BLOCKS_HERE + 1:
                    value = value + total_ref[MARGIN - 1]
            for r in range(NR):
                out_ref[r, row] = value[PORTS_DEV * r : PORTS_DEV * (r + 1)].astype(jnp.bfloat16)

    core = lax.axis_index("core")
    pl.when(core == 0)(lambda: combine(far_ref, nears_ref.at[1]))
    pl.when(core == 1)(lambda: combine(nears_ref.at[0], far_ref))


def inverse_kernel(parts_ref, taps_ref, out_ref):
    rows = parts_ref[0].astype(jnp.float32)
    for r in range(1, NR):
        rows = rows + parts_ref[r].astype(jnp.float32)
    flat = LOWS * PORTS_DEV
    low = rows[:LOWS].reshape(flat, BS)
    high = rows[LOWS:BLOCKS_HERE].reshape(flat, BS)
    low_before = jnp.concatenate([rows[BLOCKS_HERE], low[: flat - PORTS_DEV]], axis=0)
    high_before = jnp.concatenate([rows[BLOCKS_HERE + 1], high[: flat - PORTS_DEV]], axis=0)
    stacked = jnp.concatenate([low, high, low_before, high_before], axis=1)
    volts = dot_exact(stacked, taps_ref[...])
    for b in range(LOWS):
        out_ref[:, 2 * BS * b : 2 * BS * (b + 1)] = volts[PORTS_DEV * b : PORTS_DEV * (b + 1)]


def route(block, partner):
    count = NY * NZ * NC
    return lax.ppermute(block, FINE, [(i, partner(i) % count) for i in range(count)])


def windows():
    groups = []
    for core in range(NC):
        for first in range(0, NZ, 4):
            for odd in range(2):
                start = first + odd + 2 * core
                members = sorted(((z >> 1) & 1, z % NZ) for z in (start, start + 2))
                for r in range(NR):
                    groups.append(
                        [
                            ((y * NZ + z) * NC + core) * NR + r
                            for y in range(NY)
                            for _, z in members
                        ]
                    )
    return groups


def to_window(block):
    return lax.all_to_all(block, EVERY, 0, 0, tiled=True, axis_index_groups=windows())


def shards(currents, requested, block_rows, block_slots, coupling):
    bf16 = jnp.bfloat16
    next_head = route(currents[:, :BS], lambda i: i - 1)
    residues = pl.pallas_call(
        forward_kernel,
        out_shape=jax.ShapeDtypeStruct((NR, KEPT, PORTS_DEV, BS), bf16),
        in_specs=[VMEM, VMEM],
        out_specs=VMEM,
        compiler_params=PARAMS,
        name="forward",
    )(currents, next_head)
    residues = lax.all_to_all(residues, "rep", 0, 0, tiled=True)
    same = residues.transpose(1, 0, 2, 3).reshape(KEPT, PORTS, BS)
    wanted = requested.reshape(NY, NH, NM, NL * NC * 2).transpose(0, 2, 1, 3)
    wanted = wanted.reshape(NY * NM, SLOTS)
    same = lax.all_gather(same, "zhigh", axis=0)
    same, wanted = lax.optimization_barrier((same, wanted))
    other = route(same, lambda i: i ^ NC)
    same = lax.all_gather(same, "core", axis=0)
    wanted = to_window(wanted)
    other = lax.all_gather(other, "core", axis=0)
    chosen = pl.pallas_call(
        select_kernel,
        out_shape=jax.ShapeDtypeStruct((NY * NM, SLOTS, PORTS, BS), bf16),
        in_specs=[SMEM, VMEM, VMEM],
        out_specs=VMEM,
        compiler_params=PARAMS,
        name="select",
    )(wanted, same, other)
    vectors = to_window(chosen)
    whole = lambda *shape: pl.BlockSpec(shape, lambda n: (0,) * len(shape))
    total, near, far = pl.pallas_call(
        product_kernel,
        grid=(NNZ // NNZ_STEP,),
        out_shape=[
            jax.ShapeDtypeStruct((WINDOW, PORTS, BS), jnp.float32),
            jax.ShapeDtypeStruct((UP_ROWS, PORTS, BS), bf16),
            jax.ShapeDtypeStruct((UP_ROWS, PORTS, BS), bf16),
        ],
        in_specs=[
            SMEM,
            SMEM,
            whole(*vectors.shape),
            pl.BlockSpec((NNZ_STEP, BS, BS), lambda n: (n, 0, 0)),
        ],
        out_specs=[
            whole(WINDOW, PORTS, BS),
            whole(UP_ROWS, PORTS, BS),
            whole(UP_ROWS, PORTS, BS),
        ],
        compiler_params=PARAMS,
        name="products",
    )(block_rows[0], block_slots[0], vectors, coupling[0, 0])
    nears = lax.all_gather(near, "core", axis=0)
    far = route(far, lambda i: i + 1 if i % 2 else i - 1)
    parts = pl.pallas_call(
        combine_kernel,
        out_shape=jax.ShapeDtypeStruct((NR, BLOCKS_HERE + 2, PORTS_DEV, BS), bf16),
        in_specs=[VMEM, VMEM, VMEM],
        out_specs=VMEM,
        compiler_params=PARAMS,
        name="combine",
    )(total, nears, far)
    parts = lax.all_to_all(parts, "rep", 0, 0, tiled=True)
    return pl.pallas_call(
        inverse_kernel,
        out_shape=jax.ShapeDtypeStruct(currents.shape, jnp.float32),
        in_specs=[VMEM, VMEM],
        out_specs=VMEM,
        compiler_params=PARAMS,
        name="inverse",
    )(parts, jnp.asarray(inverse_matrix()))


def solution(mesh):
    grid = Mesh(mesh.devices.reshape(NY, NH, NM, NL, NC, NR), EVERY)
    placed = (
        P("rep", FINE),
        P(FINE, "rep", None, None),
        P(FINE, "rep", None),
        P(FINE, "rep", None),
        P(FINE, "rep", None, None, None),
    )
    return jax.shard_map(
        shards, mesh=grid, in_specs=placed, out_specs=P("rep", FINE), check_vma=False
    )
```

```python
import math

import jax
import jax.numpy as jnp
import numpy as np
from jax import lax
from jax.experimental import pallas as pl
from jax.experimental.pallas import tpu as pltpu
from jax.sharding import Mesh, PartitionSpec as P

ROOT_THREE = math.sqrt(3.0)
SCALE_NORM = 4.0 * math.sqrt(2.0)
LOW_PASS = (
    (1.0 + ROOT_THREE) / SCALE_NORM,
    (3.0 + ROOT_THREE) / SCALE_NORM,
    (3.0 - ROOT_THREE) / SCALE_NORM,
    (1.0 - ROOT_THREE) / SCALE_NORM,
)
HIGH_PASS = (LOW_PASS[3], -LOW_PASS[2], LOW_PASS[1], -LOW_PASS[0])

NY, NZ, NC, NR = 4, 16, 2, 4
FINE = ("y", "zhigh", "zmid", "zlow", "core")
EVERY = FINE + ("rep",)
NH, NM, NL = 4, 2, 2
BS = 128
BLOCKS_HERE = 48
MARGIN = BLOCKS_HERE // 4
WINDOW = BLOCKS_HERE + 2 * MARGIN
KEPT = BLOCKS_HERE // NR
BLOCKS_ALL = BLOCKS_HERE * NY * NZ * NC
LOWS = BLOCKS_HERE // 2
SLOTS = NH * NM * NC * 2
PORTS_DEV = 8
PORTS = PORTS_DEV * NR
NNZ = 128
NNZ_STEP = 64
UP_ROWS = MARGIN + 2
VMEM = pl.BlockSpec(memory_space=pltpu.VMEM)
SMEM = pl.BlockSpec(memory_space=pltpu.SMEM)
PARAMS = pltpu.CompilerParams(vmem_limit_bytes=48 * 1024 * 1024)


def inverse_matrix():
    taps = np.zeros((4 * BS, 2 * BS), np.float32)
    for k in range(BS):
        for odd in range(2):
            taps[k, 2 * k + odd] = LOW_PASS[odd]
            taps[BS + k, 2 * k + odd] = HIGH_PASS[odd]
            before = k - 1 if k else 2 * BS + BS - 1
            taps[before, 2 * k + odd] = LOW_PASS[2 + odd]
            before = BS + k - 1 if k else 3 * BS + BS - 1
            taps[before, 2 * k + odd] = HIGH_PASS[2 + odd]
    return taps


def dot_exact(a, b):
    return jnp.dot(a, b, precision=lax.Precision.HIGHEST, preferred_element_type=jnp.float32)


def forward_kernel(x_ref, next_ref, out_ref):
    wide = 2 * BS
    row = lax.broadcasted_iota(jnp.int32, (wide + BS, wide), 0)
    lane = lax.broadcasted_iota(jnp.int32, (wide + BS, wide), 1)
    is_low = lane < BS
    tap = row - 2 * jnp.where(is_low, lane, lane - BS)
    taps = jnp.zeros((wide + BS, wide), jnp.float32)
    for j in range(4):
        taps = jnp.where(tap == j, jnp.where(is_low, LOW_PASS[j], HIGH_PASS[j]), taps)
    here = jnp.concatenate(
        [x_ref[:, wide * b : wide * (b + 1)] for b in range(LOWS)], axis=0
    )
    after = jnp.concatenate(
        [x_ref[:, wide * b : wide * b + BS] for b in range(1, LOWS)] + [next_ref[...]], axis=0
    )
    bands = dot_exact(here, taps[:wide]) + dot_exact(after, taps[wide:])
    bands = bands.astype(jnp.bfloat16)
    for b in range(BLOCKS_HERE):
        rows = PORTS_DEV * (b % LOWS)
        lanes = BS * (b // LOWS)
        out_ref[b % NR, b // NR] = bands[rows : rows + PORTS_DEV, lanes : lanes + BS]


def select_kernel(wanted_ref, same_ref, other_ref, out_ref):
    middle = lax.axis_index("zmid")

    def one(reader, carry):
        for high in range(NH):
            found = []
            for swap, table_ref in enumerate((same_ref, other_ref)):
                place = (high * NM + (middle ^ swap)) * NC * 2
                for core in range(NC):
                    for k in range(2):
                        slot = place + 2 * core + k
                        block = jnp.maximum(wanted_ref[reader, slot], 0)
                        found.append((slot, table_ref[core, high, block >> 2]))
            for slot, block in found:
                out_ref[reader, slot] = block
        return carry

    lax.fori_loop(0, NY * NL, one, 0)


def seg_index():
    z = lax.axis_index("zhigh") * NM + lax.axis_index("zmid")
    z = z * NL + lax.axis_index("zlow")
    return (lax.axis_index("y") * NZ + z) * NC + lax.axis_index("core")


def product_kernel(rows_ref, slots_ref, vectors_ref, coupling_ref, total_ref, near_ref, far_ref):
    step = pl.program_id(0)
    edge = seg_index() * BLOCKS_HERE - MARGIN

    @pl.when(step == 0)
    def _():
        total_ref[...] = jnp.zeros_like(total_ref)

    for i in range(NNZ_STEP):
        n = step * NNZ_STEP + i
        row = rows_ref[0, n] - edge
        row = jnp.where(row < 0, row + BLOCKS_ALL, row)
        row = jnp.where(row >= BLOCKS_ALL, row - BLOCKS_ALL, row)
        slot = slots_ref[0, n]
        source = slot >> 1
        z = (source >> 1) & (NZ - 1)
        sender = (source >> 5) * NL + (z & 1)
        place = (z >> 1) * NC * 2 + (slot & 3)
        product = lax.dot_general(
            vectors_ref[sender, place],
            coupling_ref[i],
            (((1,), (1,)), ((), ())),
            preferred_element_type=jnp.float32,
        )
        total_ref[row] += product

    def margins(up_ref, down_ref):
        down_ref[:MARGIN] = total_ref[:MARGIN].astype(jnp.bfloat16)
        down_ref[MARGIN:] = jnp.zeros((2, PORTS, BS), jnp.bfloat16)
        up_ref[:MARGIN] = total_ref[MARGIN + BLOCKS_HERE :].astype(jnp.bfloat16)
        up_ref[MARGIN] = total_ref[MARGIN + LOWS - 1].astype(jnp.bfloat16)
        up_ref[MARGIN + 1] = total_ref[MARGIN + BLOCKS_HERE - 1].astype(jnp.bfloat16)

    last = step == NNZ // NNZ_STEP - 1
    core = lax.axis_index("core")
    pl.when(last & (core == 0))(lambda: margins(near_ref, far_ref))
    pl.when(last & (core == 1))(lambda: margins(far_ref, near_ref))


def combine_kernel(total_ref, nears_ref, far_ref, out_ref):
    def combine(above_ref, below_ref):
        for row in range(BLOCKS_HERE + 2):
            if row < BLOCKS_HERE:
                value = total_ref[MARGIN + row]
                if row < MARGIN:
                    value = value + above_ref[row].astype(jnp.float32)
                if row >= BLOCKS_HERE - MARGIN:
                    value = value + below_ref[row - BLOCKS_HERE + MARGIN].astype(jnp.float32)
            else:
                value = above_ref[MARGIN + row - BLOCKS_HERE].astype(jnp.float32)
                if row == BLOCKS_HERE + 1:
                    value = value + total_ref[MARGIN - 1]
            for r in range(NR):
                out_ref[r, row] = value[PORTS_DEV * r : PORTS_DEV * (r + 1)].astype(jnp.bfloat16)

    core = lax.axis_index("core")
    pl.when(core == 0)(lambda: combine(far_ref, nears_ref.at[1]))
    pl.when(core == 1)(lambda: combine(nears_ref.at[0], far_ref))


def inverse_kernel(parts_ref, taps_ref, out_ref):
    rows = parts_ref[0].astype(jnp.float32)
    for r in range(1, NR):
        rows = rows + parts_ref[r].astype(jnp.float32)
    flat = LOWS * PORTS_DEV
    low = rows[:LOWS].reshape(flat, BS)
    high = rows[LOWS:BLOCKS_HERE].reshape(flat, BS)
    low_before = jnp.concatenate([rows[BLOCKS_HERE], low[: flat - PORTS_DEV]], axis=0)
    high_before = jnp.concatenate([rows[BLOCKS_HERE + 1], high[: flat - PORTS_DEV]], axis=0)
    stacked = jnp.concatenate([low, high, low_before, high_before], axis=1)
    volts = dot_exact(stacked, taps_ref[...])
    for b in range(LOWS):
        out_ref[:, 2 * BS * b : 2 * BS * (b + 1)] = volts[PORTS_DEV * b : PORTS_DEV * (b + 1)]


def route(block, partner):
    count = NY * NZ * NC
    return lax.ppermute(block, FINE, [(i, partner(i) % count) for i in range(count)])


def windows():
    groups = []
    for core in range(NC):
        for even in range(0, NZ, 2):
            odd = (even + 1 - 2 * core) % NZ
            for r in range(NR):
                groups.append(
                    [
                        ((y * NZ + z) * NC + core) * NR + r
                        for y in range(NY)
                        for z in (even, odd)
                    ]
                )
    return groups


def two_away(i):
    core, z, y = i % NC, i // NC % NZ, i // (NC * NZ)
    step = 2 if (z >> 1) % 2 == core else -2
    return (y * NZ + (z + step) % NZ) * NC + core


def to_window(block):
    return lax.all_to_all(block, EVERY, 0, 0, tiled=True, axis_index_groups=windows())


def shards(currents, requested, block_rows, block_slots, coupling):
    bf16 = jnp.bfloat16
    next_head = route(currents[:, :BS], lambda i: i - 1)
    residues = pl.pallas_call(
        forward_kernel,
        out_shape=jax.ShapeDtypeStruct((NR, KEPT, PORTS_DEV, BS), bf16),
        in_specs=[VMEM, VMEM],
        out_specs=VMEM,
        compiler_params=PARAMS,
        name="forward",
    )(currents, next_head)
    residues = lax.all_to_all(residues, "rep", 0, 0, tiled=True)
    same = residues.transpose(1, 0, 2, 3).reshape(KEPT, PORTS, BS)
    wanted = requested.reshape(NY, NH * NM, NL, NC * 2).transpose(0, 2, 1, 3)
    wanted = wanted.reshape(NY * NL, SLOTS)
    same = lax.all_gather(same, "zhigh", axis=0)
    same, wanted = lax.optimization_barrier((same, wanted))
    other = route(same, two_away)
    same = lax.all_gather(same, "core", axis=0)
    wanted = to_window(wanted)
    other = lax.all_gather(other, "core", axis=0)
    chosen = pl.pallas_call(
        select_kernel,
        out_shape=jax.ShapeDtypeStruct((NY * NL, SLOTS, PORTS, BS), bf16),
        in_specs=[SMEM, VMEM, VMEM],
        out_specs=VMEM,
        compiler_params=PARAMS,
        name="select",
    )(wanted, same, other)
    vectors = to_window(chosen)
    whole = lambda *shape: pl.BlockSpec(shape, lambda n: (0,) * len(shape))
    total, near, far = pl.pallas_call(
        product_kernel,
        grid=(NNZ // NNZ_STEP,),
        out_shape=[
            jax.ShapeDtypeStruct((WINDOW, PORTS, BS), jnp.float32),
            jax.ShapeDtypeStruct((UP_ROWS, PORTS, BS), bf16),
            jax.ShapeDtypeStruct((UP_ROWS, PORTS, BS), bf16),
        ],
        in_specs=[
            SMEM,
            SMEM,
            whole(*vectors.shape),
            pl.BlockSpec((NNZ_STEP, BS, BS), lambda n: (n, 0, 0)),
        ],
        out_specs=[
            whole(WINDOW, PORTS, BS),
            whole(UP_ROWS, PORTS, BS),
            whole(UP_ROWS, PORTS, BS),
        ],
        compiler_params=PARAMS,
        name="products",
    )(block_rows[0], block_slots[0], vectors, coupling[0, 0])
    nears = lax.all_gather(near, "core", axis=0)
    far = route(far, lambda i: i + 1 if i % 2 else i - 1)
    parts = pl.pallas_call(
        combine_kernel,
        out_shape=jax.ShapeDtypeStruct((NR, BLOCKS_HERE + 2, PORTS_DEV, BS), bf16),
        in_specs=[VMEM, VMEM, VMEM],
        out_specs=VMEM,
        compiler_params=PARAMS,
        name="combine",
    )(total, nears, far)
    parts = lax.all_to_all(parts, "rep", 0, 0, tiled=True)
    return pl.pallas_call(
        inverse_kernel,
        out_shape=jax.ShapeDtypeStruct(currents.shape, jnp.float32),
        in_specs=[VMEM, VMEM],
        out_specs=VMEM,
        compiler_params=PARAMS,
        name="inverse",
    )(parts, jnp.asarray(inverse_matrix()))


def solution(mesh):
    grid = Mesh(mesh.devices.reshape(NY, NH, NM, NL, NC, NR), EVERY)
    placed = (
        P("rep", FINE),
        P(FINE, "rep", None, None),
        P(FINE, "rep", None),
        P(FINE, "rep", None),
        P(FINE, "rep", None, None, None),
    )
    return jax.shard_map(
        shards, mesh=grid, in_specs=placed, out_specs=P("rep", FINE), check_vma=False
    )
```

```python
import math

import jax
import jax.numpy as jnp
import numpy as np
from jax import lax
from jax.experimental import pallas as pl
from jax.experimental.pallas import tpu as pltpu
from jax.sharding import Mesh, PartitionSpec as P

ROOT_THREE = math.sqrt(3.0)
SCALE_NORM = 4.0 * math.sqrt(2.0)
LOW_PASS = (
    (1.0 + ROOT_THREE) / SCALE_NORM,
    (3.0 + ROOT_THREE) / SCALE_NORM,
    (3.0 - ROOT_THREE) / SCALE_NORM,
    (1.0 - ROOT_THREE) / SCALE_NORM,
)
HIGH_PASS = (LOW_PASS[3], -LOW_PASS[2], LOW_PASS[1], -LOW_PASS[0])

NY, NZ, NC, NR = 4, 16, 2, 4
FINE = ("y", "zhigh", "zmid", "zlow", "core")
EVERY = FINE + ("rep",)
NH, NM, NL = 4, 2, 2
BS = 128
BLOCKS_HERE = 48
MARGIN = BLOCKS_HERE // 4
WINDOW = BLOCKS_HERE + 2 * MARGIN
KEPT = BLOCKS_HERE // NR
BLOCKS_ALL = BLOCKS_HERE * NY * NZ * NC
LOWS = BLOCKS_HERE // 2
SLOTS = NH * NL * NC * 2
PORTS_DEV = 8
PORTS = PORTS_DEV * NR
NNZ = 128
UP_ROWS = MARGIN + 2
VMEM = pl.BlockSpec(memory_space=pltpu.VMEM)
SMEM = pl.BlockSpec(memory_space=pltpu.SMEM)
PARAMS = pltpu.CompilerParams(vmem_limit_bytes=48 * 1024 * 1024)


def inverse_matrix():
    taps = np.zeros((4 * BS, 2 * BS), np.float32)
    for k in range(BS):
        for odd in range(2):
            taps[k, 2 * k + odd] = LOW_PASS[odd]
            taps[BS + k, 2 * k + odd] = HIGH_PASS[odd]
            before = k - 1 if k else 2 * BS + BS - 1
            taps[before, 2 * k + odd] = LOW_PASS[2 + odd]
            before = BS + k - 1 if k else 3 * BS + BS - 1
            taps[before, 2 * k + odd] = HIGH_PASS[2 + odd]
    return taps


def dot_exact(a, b):
    return jnp.dot(a, b, precision=lax.Precision.HIGHEST, preferred_element_type=jnp.float32)


def forward_kernel(x_ref, next_ref, out_ref):
    wide = 2 * BS
    row = lax.broadcasted_iota(jnp.int32, (wide + BS, wide), 0)
    lane = lax.broadcasted_iota(jnp.int32, (wide + BS, wide), 1)
    is_low = lane < BS
    tap = row - 2 * jnp.where(is_low, lane, lane - BS)
    taps = jnp.zeros((wide + BS, wide), jnp.float32)
    for j in range(4):
        taps = jnp.where(tap == j, jnp.where(is_low, LOW_PASS[j], HIGH_PASS[j]), taps)
    here = jnp.concatenate(
        [x_ref[:, wide * b : wide * (b + 1)] for b in range(LOWS)], axis=0
    )
    after = jnp.concatenate(
        [x_ref[:, wide * b : wide * b + BS] for b in range(1, LOWS)] + [next_ref[...]], axis=0
    )
    bands = dot_exact(here, taps[:wide]) + dot_exact(after, taps[wide:])
    bands = bands.astype(jnp.bfloat16)
    for b in range(BLOCKS_HERE):
        rows = PORTS_DEV * (b % LOWS)
        lanes = BS * (b // LOWS)
        block = bands[rows : rows + PORTS_DEV, lanes : lanes + BS]
        for high in range(NH):
            out_ref[high, b % NR, b // NR] = block


def select_kernel(wanted_ref, same_ref, other_ref, out_ref):
    parity = lax.axis_index("zlow")

    def one(reader, carry):
        for high in range(NH):
            found = []
            for swap, table_ref in enumerate((same_ref, other_ref)):
                asked = (high * NL + (parity ^ swap)) * NC * 2
                for core in range(NC):
                    for k in range(2):
                        block = jnp.maximum(wanted_ref[reader, asked + 2 * core + k], 0)
                        found.append(table_ref[core, high, block >> 2])
            for i, block in enumerate(found):
                out_ref[reader, high * NL * NC * 2 + i] = block
        return carry

    lax.fori_loop(0, NY * NM, one, 0)


def seg_index():
    z = lax.axis_index("zhigh") * NM + lax.axis_index("zmid")
    z = z * NL + lax.axis_index("zlow")
    return (lax.axis_index("y") * NZ + z) * NC + lax.axis_index("core")


def product_kernel(rows_ref, slots_ref, vectors_ref, coupling_ref, total_ref, near_ref, far_ref):
    edge = seg_index() * BLOCKS_HERE - MARGIN
    parity = lax.axis_index("zlow")
    total_ref[...] = jnp.zeros_like(total_ref)
    for n in range(NNZ):
        row = rows_ref[0, n] - edge
        row = jnp.where(row < 0, row + BLOCKS_ALL, row)
        row = jnp.where(row >= BLOCKS_ALL, row - BLOCKS_ALL, row)
        slot = slots_ref[0, n]
        source = slot >> 1
        z = (source >> 1) & (NZ - 1)
        sender = (source >> 5) * NM + ((z >> 1) & 1)
        place = ((z >> 2) * NL + ((z & 1) ^ parity)) * NC * 2 + (slot & 3)
        product = lax.dot_general(
            vectors_ref[sender, place],
            coupling_ref[n],
            (((1,), (1,)), ((), ())),
            preferred_element_type=jnp.float32,
        )
        total_ref[row] += product

    def margins(up_ref, down_ref):
        down_ref[:MARGIN] = total_ref[:MARGIN].astype(jnp.bfloat16)
        down_ref[MARGIN:] = jnp.zeros((2, PORTS, BS), jnp.bfloat16)
        up_ref[:MARGIN] = total_ref[MARGIN + BLOCKS_HERE :].astype(jnp.bfloat16)
        up_ref[MARGIN] = total_ref[MARGIN + LOWS - 1].astype(jnp.bfloat16)
        up_ref[MARGIN + 1] = total_ref[MARGIN + BLOCKS_HERE - 1].astype(jnp.bfloat16)

    core = lax.axis_index("core")
    pl.when(core == 0)(lambda: margins(near_ref, far_ref))
    pl.when(core == 1)(lambda: margins(far_ref, near_ref))


def combine_kernel(total_ref, nears_ref, far_ref, out_ref):
    def combine(above_ref, below_ref):
        for row in range(BLOCKS_HERE + 2):
            if row < BLOCKS_HERE:
                value = total_ref[MARGIN + row]
                if row < MARGIN:
                    value = value + above_ref[row].astype(jnp.float32)
                if row >= BLOCKS_HERE - MARGIN:
                    value = value + below_ref[row - BLOCKS_HERE + MARGIN].astype(jnp.float32)
            else:
                value = above_ref[MARGIN + row - BLOCKS_HERE].astype(jnp.float32)
                if row == BLOCKS_HERE + 1:
                    value = value + total_ref[MARGIN - 1]
            for r in range(NR):
                out_ref[r, row] = value[PORTS_DEV * r : PORTS_DEV * (r + 1)].astype(jnp.bfloat16)

    core = lax.axis_index("core")
    pl.when(core == 0)(lambda: combine(far_ref, nears_ref.at[1]))
    pl.when(core == 1)(lambda: combine(nears_ref.at[0], far_ref))


def inverse_kernel(parts_ref, taps_ref, out_ref):
    rows = parts_ref[0].astype(jnp.float32)
    for r in range(1, NR):
        rows = rows + parts_ref[r].astype(jnp.float32)
    flat = LOWS * PORTS_DEV
    low = rows[:LOWS].reshape(flat, BS)
    high = rows[LOWS:BLOCKS_HERE].reshape(flat, BS)
    low_before = jnp.concatenate([rows[BLOCKS_HERE], low[: flat - PORTS_DEV]], axis=0)
    high_before = jnp.concatenate([rows[BLOCKS_HERE + 1], high[: flat - PORTS_DEV]], axis=0)
    stacked = jnp.concatenate([low, high, low_before, high_before], axis=1)
    volts = dot_exact(stacked, taps_ref[...])
    for b in range(LOWS):
        out_ref[:, 2 * BS * b : 2 * BS * (b + 1)] = volts[PORTS_DEV * b : PORTS_DEV * (b + 1)]


def route(block, partner):
    count = NY * NZ * NC
    return lax.ppermute(block, FINE, [(i, partner(i) % count) for i in range(count)])


def windows():
    groups = []
    for core in range(NC):
        for first in range(0, NZ, 4):
            for odd in range(2):
                start = first + odd + 2 * core
                members = sorted(((z >> 1) & 1, z % NZ) for z in (start, start + 2))
                for r in range(NR):
                    groups.append(
                        [
                            ((y * NZ + z) * NC + core) * NR + r
                            for y in range(NY)
                            for _, z in members
                        ]
                    )
    return groups


def to_window(block):
    return lax.all_to_all(block, EVERY, 0, 0, tiled=True, axis_index_groups=windows())


def shards(currents, requested, block_rows, block_slots, coupling):
    bf16 = jnp.bfloat16
    next_head = route(currents[:, :BS], lambda i: i - 1)
    residues = pl.pallas_call(
        forward_kernel,
        out_shape=jax.ShapeDtypeStruct((NH, NR, KEPT, PORTS_DEV, BS), bf16),
        in_specs=[VMEM, VMEM],
        out_specs=VMEM,
        compiler_params=PARAMS,
        name="forward",
    )(currents, next_head)
    residues = residues.reshape(NH * NR, KEPT, PORTS_DEV, BS)
    same = lax.all_to_all(residues, ("zhigh", "rep"), 0, 0, tiled=True)
    same = same.reshape(NH, NR, KEPT, PORTS_DEV, BS).transpose(0, 2, 1, 3, 4)
    same = same.reshape(NH, KEPT, PORTS, BS)
    wanted = requested.reshape(NY, NH, NM, NL * NC * 2).transpose(0, 2, 1, 3)
    wanted = wanted.reshape(NY * NM, SLOTS)
    same, wanted = lax.optimization_barrier((same, wanted))
    other = route(same, lambda i: i ^ NC)
    same = lax.all_gather(same, "core", axis=0)
    wanted = to_window(wanted)
    other = lax.all_gather(other, "core", axis=0)
    chosen = pl.pallas_call(
        select_kernel,
        out_shape=jax.ShapeDtypeStruct((NY * NM, SLOTS, PORTS, BS), bf16),
        in_specs=[SMEM, VMEM, VMEM],
        out_specs=VMEM,
        compiler_params=PARAMS,
        name="select",
    )(wanted, same, other)
    vectors = to_window(chosen)
    total, near, far = pl.pallas_call(
        product_kernel,
        out_shape=[
            jax.ShapeDtypeStruct((WINDOW, PORTS, BS), jnp.float32),
            jax.ShapeDtypeStruct((UP_ROWS, PORTS, BS), bf16),
            jax.ShapeDtypeStruct((UP_ROWS, PORTS, BS), bf16),
        ],
        in_specs=[SMEM, SMEM, VMEM, VMEM],
        out_specs=[VMEM, VMEM, VMEM],
        compiler_params=pltpu.CompilerParams(vmem_limit_bytes=24 * 1024 * 1024),
        name="products",
    )(block_rows[0], block_slots[0], vectors, coupling[0, 0])
    nears = lax.all_gather(near, "core", axis=0)
    far = route(far, lambda i: i + 1 if i % 2 else i - 1)
    parts = pl.pallas_call(
        combine_kernel,
        out_shape=jax.ShapeDtypeStruct((NR, BLOCKS_HERE + 2, PORTS_DEV, BS), bf16),
        in_specs=[VMEM, VMEM, VMEM],
        out_specs=VMEM,
        compiler_params=PARAMS,
        name="combine",
    )(total, nears, far)
    parts = lax.all_to_all(parts, "rep", 0, 0, tiled=True)
    return pl.pallas_call(
        inverse_kernel,
        out_shape=jax.ShapeDtypeStruct(currents.shape, jnp.float32),
        in_specs=[VMEM, VMEM],
        out_specs=VMEM,
        compiler_params=PARAMS,
        name="inverse",
    )(parts, jnp.asarray(inverse_matrix()))


def solution(mesh):
    grid = Mesh(mesh.devices.reshape(NY, NH, NM, NL, NC, NR), EVERY)
    placed = (
        P("rep", FINE),
        P(FINE, "rep", None, None),
        P(FINE, "rep", None),
        P(FINE, "rep", None),
        P(FINE, "rep", None, None, None),
    )
    return jax.shard_map(
        shards, mesh=grid, in_specs=placed, out_specs=P("rep", FINE), check_vma=False
    )
```

```python
import math

import jax
import jax.numpy as jnp
import numpy as np
from jax import lax
from jax.experimental import pallas as pl
from jax.experimental.pallas import tpu as pltpu
from jax.sharding import Mesh, PartitionSpec as P

ROOT_THREE = math.sqrt(3.0)
SCALE_NORM = 4.0 * math.sqrt(2.0)
LOW_PASS = (
    (1.0 + ROOT_THREE) / SCALE_NORM,
    (3.0 + ROOT_THREE) / SCALE_NORM,
    (3.0 - ROOT_THREE) / SCALE_NORM,
    (1.0 - ROOT_THREE) / SCALE_NORM,
)
HIGH_PASS = (LOW_PASS[3], -LOW_PASS[2], LOW_PASS[1], -LOW_PASS[0])

NY, NZ, NC, NR = 4, 16, 2, 4
FINE = ("y", "zhigh", "zmid", "zlow", "core")
EVERY = FINE + ("rep",)
NH, NM, NL = 4, 2, 2
BS = 128
BLOCKS_HERE = 48
MARGIN = BLOCKS_HERE // 4
WINDOW = BLOCKS_HERE + 2 * MARGIN
BLOCKS_ALL = BLOCKS_HERE * NY * NZ * NC
LOWS = BLOCKS_HERE // 2
SLOTS = NH * NM * NC * 2
PORTS_DEV = 8
PORTS = PORTS_DEV * NR
NNZ = 128
UP_ROWS = MARGIN + 2
VMEM = pl.BlockSpec(memory_space=pltpu.VMEM)
SMEM = pl.BlockSpec(memory_space=pltpu.SMEM)
PARAMS = pltpu.CompilerParams(vmem_limit_bytes=48 * 1024 * 1024)


def inverse_matrix():
    taps = np.zeros((4 * BS, 2 * BS), np.float32)
    for k in range(BS):
        for odd in range(2):
            taps[k, 2 * k + odd] = LOW_PASS[odd]
            taps[BS + k, 2 * k + odd] = HIGH_PASS[odd]
            before = k - 1 if k else 2 * BS + BS - 1
            taps[before, 2 * k + odd] = LOW_PASS[2 + odd]
            before = BS + k - 1 if k else 3 * BS + BS - 1
            taps[before, 2 * k + odd] = HIGH_PASS[2 + odd]
    return taps


def dot_exact(a, b):
    return jnp.dot(a, b, precision=lax.Precision.HIGHEST, preferred_element_type=jnp.float32)


def forward_kernel(x_ref, next_ref, out_ref):
    wide = 2 * BS
    row = lax.broadcasted_iota(jnp.int32, (wide + BS, wide), 0)
    lane = lax.broadcasted_iota(jnp.int32, (wide + BS, wide), 1)
    is_low = lane < BS
    tap = row - 2 * jnp.where(is_low, lane, lane - BS)
    taps = jnp.zeros((wide + BS, wide), jnp.float32)
    for j in range(4):
        taps = jnp.where(tap == j, jnp.where(is_low, LOW_PASS[j], HIGH_PASS[j]), taps)
    here = jnp.concatenate(
        [x_ref[:, wide * b : wide * (b + 1)] for b in range(LOWS)], axis=0
    )
    after = jnp.concatenate(
        [x_ref[:, wide * b : wide * b + BS] for b in range(1, LOWS)] + [next_ref[...]], axis=0
    )
    bands = dot_exact(here, taps[:wide]) + dot_exact(after, taps[wide:])
    bands = bands.astype(jnp.bfloat16)
    for b in range(BLOCKS_HERE):
        rows = PORTS_DEV * (b % LOWS)
        lanes = BS * (b // LOWS)
        out_ref[b] = bands[rows : rows + PORTS_DEV, lanes : lanes + BS]


def select_kernel(wanted_ref, same_ref, other_ref, out_ref):
    middle = lax.axis_index("zmid")

    def one(reader, carry):
        for high in range(NH):
            for swap, table_ref in enumerate((same_ref, other_ref)):
                place = (high * NM + (middle ^ swap)) * NC * 2
                for core in range(NC):
                    for k in range(2):
                        slot = place + 2 * core + k
                        out_ref[reader, slot] = table_ref[core, high, wanted_ref[reader, slot]]
        return carry

    lax.fori_loop(0, NY * NL * NR, one, 0)


def seg_index():
    z = lax.axis_index("zhigh") * NM + lax.axis_index("zmid")
    z = z * NL + lax.axis_index("zlow")
    return (lax.axis_index("y") * NZ + z) * NC + lax.axis_index("core")


def product_kernel(rows_ref, slots_ref, vectors_ref, coupling_ref, total_ref, near_ref, far_ref):
    edge = seg_index() * BLOCKS_HERE - MARGIN
    total_ref[...] = jnp.zeros_like(total_ref)
    for n in range(NNZ):
        row = rows_ref[0, n] - edge
        row = jnp.where(row < 0, row + BLOCKS_ALL, row)
        row = jnp.where(row >= BLOCKS_ALL, row - BLOCKS_ALL, row)
        slot = slots_ref[0, n]
        source = slot >> 1
        z = (source >> 1) & (NZ - 1)
        sender = (source >> 5) * NL + (z & 1)
        place = (z >> 1) * NC * 2 + (slot & 3)
        vector = jnp.concatenate([vectors_ref[sender, r, place] for r in range(NR)], axis=0)
        product = lax.dot_general(
            vector,
            coupling_ref[n],
            (((1,), (1,)), ((), ())),
            preferred_element_type=jnp.float32,
        )
        total_ref[row] += product

    def margins(up_ref, down_ref):
        down_ref[:MARGIN] = total_ref[:MARGIN].astype(jnp.bfloat16)
        down_ref[MARGIN:] = jnp.zeros((2, PORTS, BS), jnp.bfloat16)
        up_ref[:MARGIN] = total_ref[MARGIN + BLOCKS_HERE :].astype(jnp.bfloat16)
        up_ref[MARGIN] = total_ref[MARGIN + LOWS - 1].astype(jnp.bfloat16)
        up_ref[MARGIN + 1] = total_ref[MARGIN + BLOCKS_HERE - 1].astype(jnp.bfloat16)

    core = lax.axis_index("core")
    pl.when(core == 0)(lambda: margins(near_ref, far_ref))
    pl.when(core == 1)(lambda: margins(far_ref, near_ref))


def combine_kernel(total_ref, nears_ref, far_ref, out_ref):
    def combine(above_ref, below_ref):
        for row in range(BLOCKS_HERE + 2):
            if row < BLOCKS_HERE:
                value = total_ref[MARGIN + row]
                if row < MARGIN:
                    value = value + above_ref[row].astype(jnp.float32)
                if row >= BLOCKS_HERE - MARGIN:
                    value = value + below_ref[row - BLOCKS_HERE + MARGIN].astype(jnp.float32)
            else:
                value = above_ref[MARGIN + row - BLOCKS_HERE].astype(jnp.float32)
                if row == BLOCKS_HERE + 1:
                    value = value + total_ref[MARGIN - 1]
            for r in range(NR):
                out_ref[r, row] = value[PORTS_DEV * r : PORTS_DEV * (r + 1)].astype(jnp.bfloat16)

    core = lax.axis_index("core")
    pl.when(core == 0)(lambda: combine(far_ref, nears_ref.at[1]))
    pl.when(core == 1)(lambda: combine(nears_ref.at[0], far_ref))


def inverse_kernel(parts_ref, taps_ref, out_ref):
    rows = parts_ref[0].astype(jnp.float32)
    for r in range(1, NR):
        rows = rows + parts_ref[r].astype(jnp.float32)
    flat = LOWS * PORTS_DEV
    low = rows[:LOWS].reshape(flat, BS)
    high = rows[LOWS:BLOCKS_HERE].reshape(flat, BS)
    low_before = jnp.concatenate([rows[BLOCKS_HERE], low[: flat - PORTS_DEV]], axis=0)
    high_before = jnp.concatenate([rows[BLOCKS_HERE + 1], high[: flat - PORTS_DEV]], axis=0)
    stacked = jnp.concatenate([low, high, low_before, high_before], axis=1)
    volts = dot_exact(stacked, taps_ref[...])
    for b in range(LOWS):
        out_ref[:, 2 * BS * b : 2 * BS * (b + 1)] = volts[PORTS_DEV * b : PORTS_DEV * (b + 1)]


def route(block, partner):
    count = NY * NZ * NC
    return lax.ppermute(block, FINE, [(i, partner(i) % count) for i in range(count)])


def windows():
    groups = []
    for core in range(NC):
        for even in range(0, NZ, 2):
            odd = (even + 1 - 2 * core) % NZ
            groups.append(
                [
                    ((y * NZ + z) * NC + core) * NR + r
                    for y in range(NY)
                    for z in (even, odd)
                    for r in range(NR)
                ]
            )
    return groups


def two_away(i):
    core, z, y = i % NC, i // NC % NZ, i // (NC * NZ)
    step = 2 if (z >> 1) % 2 == core else -2
    return (y * NZ + (z + step) % NZ) * NC + core


def to_window(block):
    return lax.all_to_all(block, EVERY, 0, 0, tiled=True, axis_index_groups=windows())


def shards(currents, requested, block_rows, block_slots, coupling):
    bf16 = jnp.bfloat16
    next_head = route(currents[:, :BS], lambda i: i - 1)
    same = pl.pallas_call(
        forward_kernel,
        out_shape=jax.ShapeDtypeStruct((BLOCKS_HERE, PORTS_DEV, BS), bf16),
        in_specs=[VMEM, VMEM],
        out_specs=VMEM,
        compiler_params=PARAMS,
        name="forward",
    )(currents, next_head)
    wanted = jnp.maximum(requested, 0).reshape(NY, NH * NM, NL, NC * 2).transpose(0, 2, 1, 3)
    wanted = jnp.broadcast_to(wanted.reshape(NY, NL, 1, SLOTS), (NY, NL, NR, SLOTS))
    wanted = wanted.reshape(NY * NL * NR, SLOTS)
    same = lax.all_gather(same, "zhigh", axis=0)
    same, wanted = lax.optimization_barrier((same, wanted))
    other = route(same, two_away)
    same = lax.all_gather(same, "core", axis=0)
    wanted = to_window(wanted)
    other = lax.all_gather(other, "core", axis=0)
    chosen = pl.pallas_call(
        select_kernel,
        out_shape=jax.ShapeDtypeStruct((NY * NL * NR, SLOTS, PORTS_DEV, BS), bf16),
        in_specs=[SMEM, VMEM, VMEM],
        out_specs=VMEM,
        compiler_params=PARAMS,
        name="select",
    )(wanted, same, other)
    vectors = to_window(chosen).reshape(NY * NL, NR, SLOTS, PORTS_DEV, BS)
    total, near, far = pl.pallas_call(
        product_kernel,
        out_shape=[
            jax.ShapeDtypeStruct((WINDOW, PORTS, BS), jnp.float32),
            jax.ShapeDtypeStruct((UP_ROWS, PORTS, BS), bf16),
            jax.ShapeDtypeStruct((UP_ROWS, PORTS, BS), bf16),
        ],
        in_specs=[SMEM, SMEM, VMEM, VMEM],
        out_specs=[VMEM, VMEM, VMEM],
        compiler_params=pltpu.CompilerParams(vmem_limit_bytes=24 * 1024 * 1024),
        name="products",
    )(block_rows[0], block_slots[0], vectors, coupling[0, 0])
    nears = lax.all_gather(near, "core", axis=0)
    far = route(far, lambda i: i + 1 if i % 2 else i - 1)
    parts = pl.pallas_call(
        combine_kernel,
        out_shape=jax.ShapeDtypeStruct((NR, BLOCKS_HERE + 2, PORTS_DEV, BS), bf16),
        in_specs=[VMEM, VMEM, VMEM],
        out_specs=VMEM,
        compiler_params=PARAMS,
        name="combine",
    )(total, nears, far)
    parts = lax.all_to_all(parts, "rep", 0, 0, tiled=True)
    return pl.pallas_call(
        inverse_kernel,
        out_shape=jax.ShapeDtypeStruct(currents.shape, jnp.float32),
        in_specs=[VMEM, VMEM],
        out_specs=VMEM,
        compiler_params=PARAMS,
        name="inverse",
    )(parts, jnp.asarray(inverse_matrix()))


def solution(mesh):
    grid = Mesh(mesh.devices.reshape(NY, NH, NM, NL, NC, NR), EVERY)
    placed = (
        P("rep", FINE),
        P(FINE, "rep", None, None),
        P(FINE, "rep", None),
        P(FINE, "rep", None),
        P(FINE, "rep", None, None, None),
    )
    return jax.shard_map(
        shards, mesh=grid, in_specs=placed, out_specs=P("rep", FINE), check_vma=False
    )
```

```python
import math

import jax
import jax.numpy as jnp
import numpy as np
from jax import lax
from jax.experimental import pallas as pl
from jax.experimental.pallas import tpu as pltpu
from jax.sharding import Mesh, PartitionSpec as P

ROOT_THREE = math.sqrt(3.0)
SCALE_NORM = 4.0 * math.sqrt(2.0)
LOW_PASS = (
    (1.0 + ROOT_THREE) / SCALE_NORM,
    (3.0 + ROOT_THREE) / SCALE_NORM,
    (3.0 - ROOT_THREE) / SCALE_NORM,
    (1.0 - ROOT_THREE) / SCALE_NORM,
)
HIGH_PASS = (LOW_PASS[3], -LOW_PASS[2], LOW_PASS[1], -LOW_PASS[0])

NY, NZ, NC, NR = 4, 16, 2, 4
FINE = ("y", "zhigh", "zmid", "zlow", "core")
EVERY = FINE + ("rep",)
NH, NM, NL = 4, 2, 2
BS = 128
BLOCKS_HERE = 48
MARGIN = BLOCKS_HERE // 4
WINDOW = BLOCKS_HERE + 2 * MARGIN
BLOCKS_ALL = BLOCKS_HERE * NY * NZ * NC
LOWS = BLOCKS_HERE // 2
SLOTS = NH * NM * NC * 2
PORTS_DEV = 8
PORTS = PORTS_DEV * NR
NNZ = 128
UP_ROWS = MARGIN + 2
VMEM = pl.BlockSpec(memory_space=pltpu.VMEM)
SMEM = pl.BlockSpec(memory_space=pltpu.SMEM)
PARAMS = pltpu.CompilerParams(vmem_limit_bytes=48 * 1024 * 1024)


def inverse_matrix():
    taps = np.zeros((4 * BS, 2 * BS), np.float32)
    for k in range(BS):
        for odd in range(2):
            taps[k, 2 * k + odd] = LOW_PASS[odd]
            taps[BS + k, 2 * k + odd] = HIGH_PASS[odd]
            before = k - 1 if k else 2 * BS + BS - 1
            taps[before, 2 * k + odd] = LOW_PASS[2 + odd]
            before = BS + k - 1 if k else 3 * BS + BS - 1
            taps[before, 2 * k + odd] = HIGH_PASS[2 + odd]
    return taps


def dot_exact(a, b):
    return jnp.dot(a, b, precision=lax.Precision.HIGHEST, preferred_element_type=jnp.float32)


def forward_kernel(x_ref, out_ref):
    wide = 2 * BS
    row = lax.broadcasted_iota(jnp.int32, (wide + BS, wide), 0)
    lane = lax.broadcasted_iota(jnp.int32, (wide + BS, wide), 1)
    is_low = lane < BS
    tap = row - 2 * jnp.where(is_low, lane, lane - BS)
    taps = jnp.zeros((wide + BS, wide), jnp.float32)
    for j in range(4):
        taps = jnp.where(tap == j, jnp.where(is_low, LOW_PASS[j], HIGH_PASS[j]), taps)
    here = jnp.concatenate(
        [x_ref[:, wide * b : wide * (b + 1)] for b in range(LOWS)], axis=0
    )
    after = jnp.concatenate(
        [x_ref[:, wide * b : wide * b + BS] for b in range(1, LOWS)]
        + [jnp.zeros((PORTS_DEV, BS), jnp.float32)],
        axis=0,
    )
    bands = dot_exact(here, taps[:wide]) + dot_exact(after, taps[wide:])
    for b in range(BLOCKS_HERE):
        rows = PORTS_DEV * (b % LOWS)
        lanes = BS * (b // LOWS)
        out_ref[b] = bands[rows : rows + PORTS_DEV, lanes : lanes + BS]


def finish_kernel(bands_ref, next_ref, asked_ref, out_ref, wanted_ref):
    lane = lax.broadcasted_iota(jnp.int32, (PORTS_DEV, BS), 1)
    for b in range(BLOCKS_HERE):
        band = bands_ref[b]
        if b % LOWS == LOWS - 1:
            taps = HIGH_PASS if b // LOWS else LOW_PASS
            head = taps[2] * next_ref[:, 0:1] + taps[3] * next_ref[:, 1:2]
            band = band + jnp.where(lane == BS - 1, head, 0.0)
        out_ref[b] = band.astype(jnp.bfloat16)
    for i in range(NY * NL):
        row = jnp.maximum(asked_ref[i : i + 1], 0)
        wanted_ref[NR * i : NR * (i + 1)] = jnp.broadcast_to(row, (NR, SLOTS))


def select_kernel(wanted_ref, same_ref, other_ref, out_ref):
    middle = lax.axis_index("zmid")

    def one(reader, carry):
        for high in range(NH):
            for swap, table_ref in enumerate((same_ref, other_ref)):
                place = (high * NM + (middle ^ swap)) * NC * 2
                for core in range(NC):
                    for k in range(2):
                        slot = place + 2 * core + k
                        out_ref[reader, slot] = table_ref[core, high, wanted_ref[reader, slot]]
        return carry

    lax.fori_loop(0, NY * NL * NR, one, 0)


def seg_index():
    z = lax.axis_index("zhigh") * NM + lax.axis_index("zmid")
    z = z * NL + lax.axis_index("zlow")
    return (lax.axis_index("y") * NZ + z) * NC + lax.axis_index("core")


def product_kernel(rows_ref, slots_ref, vectors_ref, coupling_ref, total_ref, near_ref, far_ref):
    edge = seg_index() * BLOCKS_HERE - MARGIN
    total_ref[...] = jnp.zeros_like(total_ref)
    for n in range(NNZ):
        row = rows_ref[0, n] - edge
        row = jnp.where(row < 0, row + BLOCKS_ALL, row)
        row = jnp.where(row >= BLOCKS_ALL, row - BLOCKS_ALL, row)
        slot = slots_ref[0, n]
        source = slot >> 1
        z = (source >> 1) & (NZ - 1)
        sender = (source >> 5) * NL + (z & 1)
        place = (z >> 1) * NC * 2 + (slot & 3)
        vector = jnp.concatenate([vectors_ref[sender, r, place] for r in range(NR)], axis=0)
        product = lax.dot_general(
            vector,
            coupling_ref[n],
            (((1,), (1,)), ((), ())),
            preferred_element_type=jnp.float32,
        )
        total_ref[row] += product

    def margins(up_ref, down_ref):
        down_ref[:MARGIN] = total_ref[:MARGIN].astype(jnp.bfloat16)
        down_ref[MARGIN:] = jnp.zeros((2, PORTS, BS), jnp.bfloat16)
        up_ref[:MARGIN] = total_ref[MARGIN + BLOCKS_HERE :].astype(jnp.bfloat16)
        up_ref[MARGIN] = total_ref[MARGIN + LOWS - 1].astype(jnp.bfloat16)
        up_ref[MARGIN + 1] = total_ref[MARGIN + BLOCKS_HERE - 1].astype(jnp.bfloat16)

    core = lax.axis_index("core")
    pl.when(core == 0)(lambda: margins(near_ref, far_ref))
    pl.when(core == 1)(lambda: margins(far_ref, near_ref))


def combine_kernel(total_ref, nears_ref, far_ref, out_ref):
    def combine(above_ref, below_ref):
        for row in range(BLOCKS_HERE + 2):
            if row < BLOCKS_HERE:
                value = total_ref[MARGIN + row]
                if row < MARGIN:
                    value = value + above_ref[row].astype(jnp.float32)
                if row >= BLOCKS_HERE - MARGIN:
                    value = value + below_ref[row - BLOCKS_HERE + MARGIN].astype(jnp.float32)
            else:
                value = above_ref[MARGIN + row - BLOCKS_HERE].astype(jnp.float32)
                if row == BLOCKS_HERE + 1:
                    value = value + total_ref[MARGIN - 1]
            for r in range(NR):
                out_ref[r, row] = value[PORTS_DEV * r : PORTS_DEV * (r + 1)].astype(jnp.bfloat16)

    core = lax.axis_index("core")
    pl.when(core == 0)(lambda: combine(far_ref, nears_ref.at[1]))
    pl.when(core == 1)(lambda: combine(nears_ref.at[0], far_ref))


def inverse_kernel(parts_ref, taps_ref, out_ref):
    rows = parts_ref[0].astype(jnp.float32)
    for r in range(1, NR):
        rows = rows + parts_ref[r].astype(jnp.float32)
    flat = LOWS * PORTS_DEV
    low = rows[:LOWS].reshape(flat, BS)
    high = rows[LOWS:BLOCKS_HERE].reshape(flat, BS)
    low_before = jnp.concatenate([rows[BLOCKS_HERE], low[: flat - PORTS_DEV]], axis=0)
    high_before = jnp.concatenate([rows[BLOCKS_HERE + 1], high[: flat - PORTS_DEV]], axis=0)
    stacked = jnp.concatenate([low, high, low_before, high_before], axis=1)
    volts = dot_exact(stacked, taps_ref[...])
    for b in range(LOWS):
        out_ref[:, 2 * BS * b : 2 * BS * (b + 1)] = volts[PORTS_DEV * b : PORTS_DEV * (b + 1)]


def route(block, partner):
    count = NY * NZ * NC
    return lax.ppermute(block, FINE, [(i, partner(i) % count) for i in range(count)])


def windows():
    groups = []
    for core in range(NC):
        for even in range(0, NZ, 2):
            odd = (even + 1 - 2 * core) % NZ
            groups.append(
                [
                    ((y * NZ + z) * NC + core) * NR + r
                    for y in range(NY)
                    for z in (even, odd)
                    for r in range(NR)
                ]
            )
    return groups


def two_away(i):
    core, z, y = i % NC, i // NC % NZ, i // (NC * NZ)
    step = 2 if (z >> 1) % 2 == core else -2
    return (y * NZ + (z + step) % NZ) * NC + core


def to_window(block):
    return lax.all_to_all(block, EVERY, 0, 0, tiled=True, axis_index_groups=windows())


def shards(currents, requested, block_rows, block_slots, coupling):
    bf16 = jnp.bfloat16
    next_head = route(currents[:, :BS], lambda i: i - 1)
    bands = pl.pallas_call(
        forward_kernel,
        out_shape=jax.ShapeDtypeStruct((BLOCKS_HERE, PORTS_DEV, BS), jnp.float32),
        in_specs=[VMEM],
        out_specs=VMEM,
        compiler_params=PARAMS,
        name="forward",
    )(currents)
    asked = requested.reshape(NY, NH * NM, NL, NC * 2).transpose(0, 2, 1, 3)
    asked = asked.reshape(NY * NL, SLOTS)
    same, wanted = pl.pallas_call(
        finish_kernel,
        out_shape=[
            jax.ShapeDtypeStruct((BLOCKS_HERE, PORTS_DEV, BS), bf16),
            jax.ShapeDtypeStruct((NY * NL * NR, SLOTS), jnp.int32),
        ],
        in_specs=[VMEM, VMEM, VMEM],
        out_specs=[VMEM, VMEM],
        compiler_params=PARAMS,
        name="finish",
    )(bands, next_head, asked)
    same = lax.all_gather(same, "zhigh", axis=0)
    same, wanted = lax.optimization_barrier((same, wanted))
    other = route(same, two_away)
    same = lax.all_gather(same, "core", axis=0)
    wanted = to_window(wanted)
    other = lax.all_gather(other, "core", axis=0)
    chosen = pl.pallas_call(
        select_kernel,
        out_shape=jax.ShapeDtypeStruct((NY * NL * NR, SLOTS, PORTS_DEV, BS), bf16),
        in_specs=[SMEM, VMEM, VMEM],
        out_specs=VMEM,
        compiler_params=PARAMS,
        name="select",
    )(wanted, same, other)
    vectors = to_window(chosen).reshape(NY * NL, NR, SLOTS, PORTS_DEV, BS)
    total, near, far = pl.pallas_call(
        product_kernel,
        out_shape=[
            jax.ShapeDtypeStruct((WINDOW, PORTS, BS), jnp.float32),
            jax.ShapeDtypeStruct((UP_ROWS, PORTS, BS), bf16),
            jax.ShapeDtypeStruct((UP_ROWS, PORTS, BS), bf16),
        ],
        in_specs=[SMEM, SMEM, VMEM, VMEM],
        out_specs=[VMEM, VMEM, VMEM],
        compiler_params=pltpu.CompilerParams(vmem_limit_bytes=24 * 1024 * 1024),
        name="products",
    )(block_rows[0], block_slots[0], vectors, coupling[0, 0])
    nears = lax.all_gather(near, "core", axis=0)
    far = route(far, lambda i: i + 1 if i % 2 else i - 1)
    parts = pl.pallas_call(
        combine_kernel,
        out_shape=jax.ShapeDtypeStruct((NR, BLOCKS_HERE + 2, PORTS_DEV, BS), bf16),
        in_specs=[VMEM, VMEM, VMEM],
        out_specs=VMEM,
        compiler_params=PARAMS,
        name="combine",
    )(total, nears, far)
    parts = lax.all_to_all(parts, "rep", 0, 0, tiled=True)
    return pl.pallas_call(
        inverse_kernel,
        out_shape=jax.ShapeDtypeStruct(currents.shape, jnp.float32),
        in_specs=[VMEM, VMEM],
        out_specs=VMEM,
        compiler_params=PARAMS,
        name="inverse",
    )(parts, jnp.asarray(inverse_matrix()))


def solution(mesh):
    grid = Mesh(mesh.devices.reshape(NY, NH, NM, NL, NC, NR), EVERY)
    placed = (
        P("rep", FINE),
        P(FINE, "rep", None, None),
        P(FINE, "rep", None),
        P(FINE, "rep", None),
        P(FINE, "rep", None, None, None),
    )
    return jax.shard_map(
        shards, mesh=grid, in_specs=placed, out_specs=P("rep", FINE), check_vma=False
    )
```

```python
import math

import jax
import jax.numpy as jnp
import numpy as np
from jax import lax
from jax.experimental import pallas as pl
from jax.experimental.pallas import tpu as pltpu
from jax.sharding import Mesh, PartitionSpec as P

ROOT_THREE = math.sqrt(3.0)
SCALE_NORM = 4.0 * math.sqrt(2.0)
LOW_PASS = (
    (1.0 + ROOT_THREE) / SCALE_NORM,
    (3.0 + ROOT_THREE) / SCALE_NORM,
    (3.0 - ROOT_THREE) / SCALE_NORM,
    (1.0 - ROOT_THREE) / SCALE_NORM,
)
HIGH_PASS = (LOW_PASS[3], -LOW_PASS[2], LOW_PASS[1], -LOW_PASS[0])

NY, NZ, NC, NR = 4, 16, 2, 4
FINE = ("y", "zhigh", "zmid", "zlow", "core")
EVERY = FINE + ("rep",)
NH, NM, NL = 4, 2, 2
BS = 128
BLOCKS_HERE = 48
MARGIN = BLOCKS_HERE // 4
WINDOW = BLOCKS_HERE + 2 * MARGIN
BLOCKS_ALL = BLOCKS_HERE * NY * NZ * NC
LOWS = BLOCKS_HERE // 2
SLOTS = NH * NM * NC * 2
PORTS_DEV = 8
PORTS = PORTS_DEV * NR
NNZ = 128
UP_ROWS = MARGIN + 2
VMEM = pl.BlockSpec(memory_space=pltpu.VMEM)
SMEM = pl.BlockSpec(memory_space=pltpu.SMEM)
PARAMS = pltpu.CompilerParams(vmem_limit_bytes=48 * 1024 * 1024)


def inverse_matrix():
    taps = np.zeros((4 * BS, 2 * BS), np.float32)
    for k in range(BS):
        for odd in range(2):
            taps[k, 2 * k + odd] = LOW_PASS[odd]
            taps[BS + k, 2 * k + odd] = HIGH_PASS[odd]
            before = k - 1 if k else 2 * BS + BS - 1
            taps[before, 2 * k + odd] = LOW_PASS[2 + odd]
            before = BS + k - 1 if k else 3 * BS + BS - 1
            taps[before, 2 * k + odd] = HIGH_PASS[2 + odd]
    return taps


def dot_exact(a, b):
    return jnp.dot(a, b, precision=lax.Precision.HIGHEST, preferred_element_type=jnp.float32)


def forward_kernel(x_ref, out_ref):
    wide = 2 * BS
    row = lax.broadcasted_iota(jnp.int32, (wide + BS, wide), 0)
    lane = lax.broadcasted_iota(jnp.int32, (wide + BS, wide), 1)
    is_low = lane < BS
    tap = row - 2 * jnp.where(is_low, lane, lane - BS)
    taps = jnp.zeros((wide + BS, wide), jnp.float32)
    for j in range(4):
        taps = jnp.where(tap == j, jnp.where(is_low, LOW_PASS[j], HIGH_PASS[j]), taps)
    here = jnp.concatenate(
        [x_ref[:, wide * b : wide * (b + 1)] for b in range(LOWS)], axis=0
    )
    after = jnp.concatenate(
        [x_ref[:, wide * b : wide * b + BS] for b in range(1, LOWS)]
        + [jnp.zeros((PORTS_DEV, BS), jnp.float32)],
        axis=0,
    )
    bands = dot_exact(here, taps[:wide]) + dot_exact(after, taps[wide:])
    for b in range(BLOCKS_HERE):
        rows = PORTS_DEV * (b % LOWS)
        lanes = BS * (b // LOWS)
        out_ref[b] = bands[rows : rows + PORTS_DEV, lanes : lanes + BS]


def finish_kernel(bands_ref, next_ref, asked_ref, out_ref, wanted_ref):
    lane = lax.broadcasted_iota(jnp.int32, (PORTS_DEV, BS), 1)
    for b in range(BLOCKS_HERE):
        band = bands_ref[b]
        if b % LOWS == LOWS - 1:
            taps = HIGH_PASS if b // LOWS else LOW_PASS
            head = taps[2] * next_ref[:, 0:1] + taps[3] * next_ref[:, 1:2]
            band = band + jnp.where(lane == BS - 1, head, 0.0)
        out_ref[b] = band.astype(jnp.bfloat16)
    for i in range(NY * NL):
        row = jnp.maximum(asked_ref[i : i + 1], 0)
        wanted_ref[NR * i : NR * (i + 1)] = jnp.broadcast_to(row, (NR, SLOTS))


def select_kernel(wanted_ref, same_ref, other_ref, out_ref):
    middle = lax.axis_index("zmid")

    def one(reader, carry):
        for high in range(NH):
            for swap, table_ref in enumerate((same_ref, other_ref)):
                place = (high * NM + (middle ^ swap)) * NC * 2
                for core in range(NC):
                    for k in range(2):
                        slot = place + 2 * core + k
                        out_ref[reader, slot] = table_ref[core, high, wanted_ref[reader, slot]]
        return carry

    lax.fori_loop(0, NY * NL * NR, one, 0)


def seg_index():
    z = lax.axis_index("zhigh") * NM + lax.axis_index("zmid")
    z = z * NL + lax.axis_index("zlow")
    return (lax.axis_index("y") * NZ + z) * NC + lax.axis_index("core")


def product_kernel(rows_ref, slots_ref, vectors_ref, coupling_ref, parts_ref, total_ref):
    edge = seg_index() * BLOCKS_HERE - MARGIN
    total_ref[...] = jnp.zeros_like(total_ref)
    for n in range(NNZ):
        row = rows_ref[0, n] - edge
        row = jnp.where(row < 0, row + BLOCKS_ALL, row)
        row = jnp.where(row >= BLOCKS_ALL, row - BLOCKS_ALL, row)
        slot = slots_ref[0, n]
        source = slot >> 1
        z = (source >> 1) & (NZ - 1)
        sender = (source >> 5) * NL + (z & 1)
        place = (z >> 1) * NC * 2 + (slot & 3)
        vector = jnp.concatenate([vectors_ref[sender, r, place] for r in range(NR)], axis=0)
        product = lax.dot_general(
            vector,
            coupling_ref[n],
            (((1,), (1,)), ((), ())),
            preferred_element_type=jnp.float32,
        )
        total_ref[row] += product

    for r in range(NR):
        for row in range(WINDOW):
            parts_ref[r, row] = total_ref[row, PORTS_DEV * r : PORTS_DEV * (r + 1)].astype(
                jnp.bfloat16
            )


def sum_kernel(parts_ref, total_ref, near_ref, far_ref):
    total = parts_ref[0].astype(jnp.float32)
    for r in range(1, NR):
        total = total + parts_ref[r].astype(jnp.float32)
    total_ref[...] = total

    def margins(up_ref, down_ref):
        down_ref[:MARGIN] = total_ref[:MARGIN]
        down_ref[MARGIN:] = jnp.zeros((2, PORTS_DEV, BS), jnp.float32)
        up_ref[:MARGIN] = total_ref[MARGIN + BLOCKS_HERE :]
        up_ref[MARGIN] = total_ref[MARGIN + LOWS - 1]
        up_ref[MARGIN + 1] = total_ref[MARGIN + BLOCKS_HERE - 1]

    core = lax.axis_index("core")
    pl.when(core == 0)(lambda: margins(near_ref, far_ref))
    pl.when(core == 1)(lambda: margins(far_ref, near_ref))


def inverse_kernel(total_ref, nears_ref, far_ref, taps_ref, out_ref):
    first = lax.axis_index("core") == 0
    above = jnp.where(first, far_ref[...], nears_ref[0])
    below = jnp.where(first, nears_ref[1], far_ref[...])
    own = total_ref[MARGIN : MARGIN + BLOCKS_HERE]
    rows = jnp.concatenate(
        [
            own[:MARGIN] + above[:MARGIN],
            own[MARGIN : BLOCKS_HERE - MARGIN],
            own[BLOCKS_HERE - MARGIN :] + below[:MARGIN],
        ],
        axis=0,
    )
    low_edge = above[MARGIN]
    high_edge = above[MARGIN + 1] + total_ref[MARGIN - 1]
    flat = LOWS * PORTS_DEV
    low = rows[:LOWS].reshape(flat, BS)
    high = rows[LOWS:BLOCKS_HERE].reshape(flat, BS)
    low_before = jnp.concatenate([low_edge, low[: flat - PORTS_DEV]], axis=0)
    high_before = jnp.concatenate([high_edge, high[: flat - PORTS_DEV]], axis=0)
    stacked = jnp.concatenate([low, high, low_before, high_before], axis=1)
    volts = dot_exact(stacked, taps_ref[...])
    for b in range(LOWS):
        out_ref[:, 2 * BS * b : 2 * BS * (b + 1)] = volts[PORTS_DEV * b : PORTS_DEV * (b + 1)]


def route(block, partner):
    count = NY * NZ * NC
    return lax.ppermute(block, FINE, [(i, partner(i) % count) for i in range(count)])


def windows():
    groups = []
    for core in range(NC):
        for even in range(0, NZ, 2):
            odd = (even + 1 - 2 * core) % NZ
            groups.append(
                [
                    ((y * NZ + z) * NC + core) * NR + r
                    for y in range(NY)
                    for z in (even, odd)
                    for r in range(NR)
                ]
            )
    return groups


def two_away(i):
    core, z, y = i % NC, i // NC % NZ, i // (NC * NZ)
    step = 2 if (z >> 1) % 2 == core else -2
    return (y * NZ + (z + step) % NZ) * NC + core


def to_window(block):
    return lax.all_to_all(block, EVERY, 0, 0, tiled=True, axis_index_groups=windows())


def shards(currents, requested, block_rows, block_slots, coupling):
    bf16 = jnp.bfloat16
    next_head = route(currents[:, :BS], lambda i: i - 1)
    bands = pl.pallas_call(
        forward_kernel,
        out_shape=jax.ShapeDtypeStruct((BLOCKS_HERE, PORTS_DEV, BS), jnp.float32),
        in_specs=[VMEM],
        out_specs=VMEM,
        compiler_params=PARAMS,
        name="forward",
    )(currents)
    asked = requested.reshape(NY, NH * NM, NL, NC * 2).transpose(0, 2, 1, 3)
    asked = asked.reshape(NY * NL, SLOTS)
    same, wanted = pl.pallas_call(
        finish_kernel,
        out_shape=[
            jax.ShapeDtypeStruct((BLOCKS_HERE, PORTS_DEV, BS), bf16),
            jax.ShapeDtypeStruct((NY * NL * NR, SLOTS), jnp.int32),
        ],
        in_specs=[VMEM, VMEM, VMEM],
        out_specs=[VMEM, VMEM],
        compiler_params=PARAMS,
        name="finish",
    )(bands, next_head, asked)
    same = lax.all_gather(same, "zhigh", axis=0)
    same, wanted = lax.optimization_barrier((same, wanted))
    other = route(same, two_away)
    same = lax.all_gather(same, "core", axis=0)
    wanted = to_window(wanted)
    other = lax.all_gather(other, "core", axis=0)
    chosen = pl.pallas_call(
        select_kernel,
        out_shape=jax.ShapeDtypeStruct((NY * NL * NR, SLOTS, PORTS_DEV, BS), bf16),
        in_specs=[SMEM, VMEM, VMEM],
        out_specs=VMEM,
        compiler_params=PARAMS,
        name="select",
    )(wanted, same, other)
    vectors = to_window(chosen).reshape(NY * NL, NR, SLOTS, PORTS_DEV, BS)
    parts = pl.pallas_call(
        product_kernel,
        out_shape=jax.ShapeDtypeStruct((NR, WINDOW, PORTS_DEV, BS), bf16),
        in_specs=[SMEM, SMEM, VMEM, VMEM],
        out_specs=VMEM,
        scratch_shapes=[pltpu.VMEM((WINDOW, PORTS, BS), jnp.float32)],
        compiler_params=pltpu.CompilerParams(vmem_limit_bytes=24 * 1024 * 1024),
        name="products",
    )(block_rows[0], block_slots[0], vectors, coupling[0, 0])
    parts = lax.all_to_all(parts, "rep", 0, 0, tiled=True)
    total, near, far = pl.pallas_call(
        sum_kernel,
        out_shape=[
            jax.ShapeDtypeStruct((WINDOW, PORTS_DEV, BS), jnp.float32),
            jax.ShapeDtypeStruct((UP_ROWS, PORTS_DEV, BS), jnp.float32),
            jax.ShapeDtypeStruct((UP_ROWS, PORTS_DEV, BS), jnp.float32),
        ],
        in_specs=[VMEM],
        out_specs=[VMEM, VMEM, VMEM],
        compiler_params=PARAMS,
        name="sums",
    )(parts)
    nears = lax.all_gather(near, "core", axis=0)
    far = route(far, lambda i: i + 1 if i % 2 else i - 1)
    return pl.pallas_call(
        inverse_kernel,
        out_shape=jax.ShapeDtypeStruct(currents.shape, jnp.float32),
        in_specs=[VMEM, VMEM, VMEM, VMEM],
        out_specs=VMEM,
        compiler_params=PARAMS,
        name="inverse",
    )(total, nears, far, jnp.asarray(inverse_matrix()))


def solution(mesh):
    grid = Mesh(mesh.devices.reshape(NY, NH, NM, NL, NC, NR), EVERY)
    placed = (
        P("rep", FINE),
        P(FINE, "rep", None, None),
        P(FINE, "rep", None),
        P(FINE, "rep", None),
        P(FINE, "rep", None, None, None),
    )
    return jax.shard_map(
        shards, mesh=grid, in_specs=placed, out_specs=P("rep", FINE), check_vma=False
    )
```

```python
import math

import jax
import jax.numpy as jnp
import numpy as np
from jax import lax
from jax.experimental import pallas as pl
from jax.experimental.pallas import tpu as pltpu
from jax.sharding import Mesh, PartitionSpec as P

ROOT_THREE = math.sqrt(3.0)
SCALE_NORM = 4.0 * math.sqrt(2.0)
LOW_PASS = (
    (1.0 + ROOT_THREE) / SCALE_NORM,
    (3.0 + ROOT_THREE) / SCALE_NORM,
    (3.0 - ROOT_THREE) / SCALE_NORM,
    (1.0 - ROOT_THREE) / SCALE_NORM,
)
HIGH_PASS = (LOW_PASS[3], -LOW_PASS[2], LOW_PASS[1], -LOW_PASS[0])

NY, NZ, NC, NR = 4, 16, 2, 4
FINE = ("y", "zhigh", "zmid", "zlow", "core")
EVERY = FINE + ("rep",)
NH, NM, NL = 4, 2, 2
BS = 128
BLOCKS_HERE = 48
MARGIN = BLOCKS_HERE // 4
WINDOW = BLOCKS_HERE + 2 * MARGIN
BLOCKS_ALL = BLOCKS_HERE * NY * NZ * NC
LOWS = BLOCKS_HERE // 2
SLOTS = NH * NM * NC * 2
PORTS_DEV = 8
PORTS = PORTS_DEV * NR
NNZ = 128
UP_ROWS = MARGIN + 2
VMEM = pl.BlockSpec(memory_space=pltpu.VMEM)
SMEM = pl.BlockSpec(memory_space=pltpu.SMEM)
PARAMS = pltpu.CompilerParams(vmem_limit_bytes=48 * 1024 * 1024)


def inverse_matrix():
    taps = np.zeros((2 * BS, 2 * BS), np.float32)
    for k in range(BS):
        for odd in range(2):
            taps[k, 2 * k + odd] = LOW_PASS[odd]
            taps[BS + k, 2 * k + odd] = HIGH_PASS[odd]
            if k:
                taps[k - 1, 2 * k + odd] = LOW_PASS[2 + odd]
                taps[BS + k - 1, 2 * k + odd] = HIGH_PASS[2 + odd]
    return taps


def dot_exact(a, b):
    return jnp.dot(a, b, precision=lax.Precision.HIGHEST, preferred_element_type=jnp.float32)


def forward_kernel(x_ref, asked_ref, out_ref, wanted_ref):
    asked = jnp.maximum(asked_ref[...], 0)
    for i in range(NY * NL * NR):
        wanted_ref[i] = asked
    wide = 2 * BS
    row = lax.broadcasted_iota(jnp.int32, (wide + BS, wide), 0)
    lane = lax.broadcasted_iota(jnp.int32, (wide + BS, wide), 1)
    is_low = lane < BS
    tap = row - 2 * jnp.where(is_low, lane, lane - BS)
    taps = jnp.zeros((wide + BS, wide), jnp.float32)
    for j in range(4):
        taps = jnp.where(tap == j, jnp.where(is_low, LOW_PASS[j], HIGH_PASS[j]), taps)
    here = jnp.concatenate(
        [x_ref[:, wide * b : wide * (b + 1)] for b in range(LOWS)], axis=0
    )
    after = jnp.concatenate(
        [x_ref[:, wide * b : wide * b + BS] for b in range(1, LOWS)]
        + [jnp.zeros((PORTS_DEV, BS), jnp.float32)],
        axis=0,
    )
    bands = dot_exact(here, taps[:wide]) + dot_exact(after, taps[wide:])
    for b in range(BLOCKS_HERE):
        rows = PORTS_DEV * (b % LOWS)
        lanes = BS * (b // LOWS)
        out_ref[b] = bands[rows : rows + PORTS_DEV, lanes : lanes + BS]


def finish_kernel(bands_ref, next_ref, out_ref):
    lane = lax.broadcasted_iota(jnp.int32, (PORTS_DEV, BS), 1)
    for b in range(BLOCKS_HERE):
        band = bands_ref[b]
        if b % LOWS == LOWS - 1:
            taps = HIGH_PASS if b // LOWS else LOW_PASS
            head = taps[2] * next_ref[:, 0:1] + taps[3] * next_ref[:, 1:2]
            band = band + jnp.where(lane == BS - 1, head, 0.0)
        out_ref[b] = band.astype(jnp.bfloat16)


def select_kernel(wanted_ref, same_ref, other_ref, out_ref):
    middle = lax.axis_index("zmid")
    corner = (lax.axis_index("y") * NZ + lax.axis_index("zlow")) * NC

    def one(reader, carry):
        for high in range(NH):
            for swap, table_ref in enumerate((same_ref, other_ref)):
                pair = high * NM + (middle ^ swap)
                for core in range(NC):
                    source = corner + pair * NL * NC + core
                    for k in range(2):
                        block = wanted_ref[reader, k, source]
                        slot = (pair * NC + core) * 2 + k
                        out_ref[reader, slot] = table_ref[core, high, block]
        return carry

    lax.fori_loop(0, NY * NL * NR, one, 0)


def seg_index():
    z = lax.axis_index("zhigh") * NM + lax.axis_index("zmid")
    z = z * NL + lax.axis_index("zlow")
    return (lax.axis_index("y") * NZ + z) * NC + lax.axis_index("core")


def product_kernel(rows_ref, slots_ref, vectors_ref, coupling_ref, total_ref, near_ref, far_ref):
    edge = seg_index() * BLOCKS_HERE - MARGIN
    total_ref[...] = jnp.zeros_like(total_ref)
    for n in range(NNZ):
        row = rows_ref[0, n] - edge
        row = jnp.where(row < 0, row + BLOCKS_ALL, row)
        row = jnp.where(row >= BLOCKS_ALL, row - BLOCKS_ALL, row)
        slot = slots_ref[0, n]
        source = slot >> 1
        z = (source >> 1) & (NZ - 1)
        sender = (source >> 5) * NL + (z & 1)
        place = (z >> 1) * NC * 2 + (slot & 3)
        vector = jnp.concatenate([vectors_ref[sender, r, place] for r in range(NR)], axis=0)
        product = lax.dot_general(
            vector,
            coupling_ref[n],
            (((1,), (1,)), ((), ())),
            preferred_element_type=jnp.float32,
        )
        total_ref[row] += product

    def margins(up_ref, down_ref):
        down_ref[:MARGIN] = total_ref[:MARGIN].astype(jnp.bfloat16)
        down_ref[MARGIN:] = jnp.zeros((2, PORTS, BS), jnp.bfloat16)
        up_ref[:MARGIN] = total_ref[MARGIN + BLOCKS_HERE :].astype(jnp.bfloat16)
        up_ref[MARGIN] = total_ref[MARGIN + LOWS - 1].astype(jnp.bfloat16)
        up_ref[MARGIN + 1] = total_ref[MARGIN + BLOCKS_HERE - 1].astype(jnp.bfloat16)

    core = lax.axis_index("core")
    pl.when(core == 0)(lambda: margins(near_ref, far_ref))
    pl.when(core == 1)(lambda: margins(far_ref, near_ref))


def combine_kernel(total_ref, nears_ref, far_ref, out_ref):
    def combine(above_ref, below_ref):
        for row in range(BLOCKS_HERE + 2):
            if row < BLOCKS_HERE:
                value = total_ref[MARGIN + row]
                if row < MARGIN:
                    value = value + above_ref[row].astype(jnp.float32)
                if row >= BLOCKS_HERE - MARGIN:
                    value = value + below_ref[row - BLOCKS_HERE + MARGIN].astype(jnp.float32)
            else:
                value = above_ref[MARGIN + row - BLOCKS_HERE].astype(jnp.float32)
                if row == BLOCKS_HERE + 1:
                    value = value + total_ref[MARGIN - 1]
            for r in range(NR):
                out_ref[r, row] = value[PORTS_DEV * r : PORTS_DEV * (r + 1)].astype(jnp.bfloat16)

    core = lax.axis_index("core")
    pl.when(core == 0)(lambda: combine(far_ref, nears_ref.at[1]))
    pl.when(core == 1)(lambda: combine(nears_ref.at[0], far_ref))


def inverse_kernel(parts_ref, taps_ref, out_ref):
    rows = parts_ref[0].astype(jnp.float32)
    for r in range(1, NR):
        rows = rows + parts_ref[r].astype(jnp.float32)
    flat = LOWS * PORTS_DEV
    low = rows[:LOWS].reshape(flat, BS)
    high = rows[LOWS:BLOCKS_HERE].reshape(flat, BS)
    low_before = jnp.concatenate([rows[BLOCKS_HERE], low[: flat - PORTS_DEV]], axis=0)
    high_before = jnp.concatenate([rows[BLOCKS_HERE + 1], high[: flat - PORTS_DEV]], axis=0)
    volts = dot_exact(jnp.concatenate([low, high], axis=1), taps_ref[...])
    low_last, high_last = low_before[:, BS - 1 :], high_before[:, BS - 1 :]
    lane = lax.broadcasted_iota(jnp.int32, (flat, BS), 1)
    edge = jnp.where(lane == 0, LOW_PASS[2] * low_last + HIGH_PASS[2] * high_last, 0.0)
    edge = jnp.where(lane == 1, LOW_PASS[3] * low_last + HIGH_PASS[3] * high_last, edge)
    near_edge = volts[:, :BS] + edge
    for b in range(LOWS):
        rows = slice(PORTS_DEV * b, PORTS_DEV * (b + 1))
        out_ref[:, 2 * BS * b : 2 * BS * b + BS] = near_edge[rows]
        out_ref[:, 2 * BS * b + BS : 2 * BS * (b + 1)] = volts[rows, BS:]


def route(block, partner):
    count = NY * NZ * NC
    return lax.ppermute(block, FINE, [(i, partner(i) % count) for i in range(count)])


def windows():
    groups = []
    for core in range(NC):
        for even in range(0, NZ, 2):
            odd = (even + 1 - 2 * core) % NZ
            groups.append(
                [
                    ((y * NZ + z) * NC + core) * NR + r
                    for y in range(NY)
                    for z in (even, odd)
                    for r in range(NR)
                ]
            )
    return groups


def two_away(i):
    core, z, y = i % NC, i // NC % NZ, i // (NC * NZ)
    step = 2 if (z >> 1) % 2 == core else -2
    return (y * NZ + (z + step) % NZ) * NC + core


def to_window(block):
    return lax.all_to_all(block, EVERY, 0, 0, tiled=True, axis_index_groups=windows())


def shards(currents, requested, block_rows, block_slots, coupling):
    bf16 = jnp.bfloat16
    next_head = route(currents[:, :BS], lambda i: i - 1)
    bands, wanted = pl.pallas_call(
        forward_kernel,
        out_shape=[
            jax.ShapeDtypeStruct((BLOCKS_HERE, PORTS_DEV, BS), jnp.float32),
            jax.ShapeDtypeStruct((NY * NL * NR,) + requested.shape[:1:-1], jnp.int32),
        ],
        in_specs=[VMEM, VMEM],
        out_specs=[VMEM, VMEM],
        compiler_params=PARAMS,
        name="forward",
    )(currents, requested[0, 0].T)
    same = pl.pallas_call(
        finish_kernel,
        out_shape=jax.ShapeDtypeStruct((BLOCKS_HERE, PORTS_DEV, BS), bf16),
        in_specs=[VMEM, VMEM],
        out_specs=VMEM,
        compiler_params=PARAMS,
        name="finish",
    )(bands, next_head)
    same = lax.all_gather(same, "zhigh", axis=0)
    same, wanted = lax.optimization_barrier((same, wanted))
    other = route(same, two_away)
    same = lax.all_gather(same, "core", axis=0)
    wanted = to_window(wanted)
    other = lax.all_gather(other, "core", axis=0)
    chosen = pl.pallas_call(
        select_kernel,
        out_shape=jax.ShapeDtypeStruct((NY * NL * NR, SLOTS, PORTS_DEV, BS), bf16),
        in_specs=[SMEM, VMEM, VMEM],
        out_specs=VMEM,
        compiler_params=PARAMS,
        name="select",
    )(wanted, same, other)
    vectors = to_window(chosen).reshape(NY * NL, NR, SLOTS, PORTS_DEV, BS)
    total, near, far = pl.pallas_call(
        product_kernel,
        out_shape=[
            jax.ShapeDtypeStruct((WINDOW, PORTS, BS), jnp.float32),
            jax.ShapeDtypeStruct((UP_ROWS, PORTS, BS), bf16),
            jax.ShapeDtypeStruct((UP_ROWS, PORTS, BS), bf16),
        ],
        in_specs=[SMEM, SMEM, VMEM, VMEM],
        out_specs=[VMEM, VMEM, VMEM],
        compiler_params=pltpu.CompilerParams(vmem_limit_bytes=24 * 1024 * 1024),
        name="products",
    )(block_rows[0], block_slots[0], vectors, coupling[0, 0])
    nears = lax.all_gather(near, "core", axis=0)
    far = route(far, lambda i: i + 1 if i % 2 else i - 1)
    parts = pl.pallas_call(
        combine_kernel,
        out_shape=jax.ShapeDtypeStruct((NR, BLOCKS_HERE + 2, PORTS_DEV, BS), bf16),
        in_specs=[VMEM, VMEM, VMEM],
        out_specs=VMEM,
        compiler_params=PARAMS,
        name="combine",
    )(total, nears, far)
    parts = lax.all_to_all(parts, "rep", 0, 0, tiled=True)
    return pl.pallas_call(
        inverse_kernel,
        out_shape=jax.ShapeDtypeStruct(currents.shape, jnp.float32),
        in_specs=[VMEM, VMEM],
        out_specs=VMEM,
        compiler_params=PARAMS,
        name="inverse",
    )(parts, jnp.asarray(inverse_matrix()))


def solution(mesh):
    grid = Mesh(mesh.devices.reshape(NY, NH, NM, NL, NC, NR), EVERY)
    placed = (
        P("rep", FINE),
        P(FINE, "rep", None, None),
        P(FINE, "rep", None),
        P(FINE, "rep", None),
        P(FINE, "rep", None, None, None),
    )
    return jax.shard_map(
        shards, mesh=grid, in_specs=placed, out_specs=P("rep", FINE), check_vma=False
    )
```

```python
import math

import jax
import jax.numpy as jnp
import numpy as np
from jax import lax
from jax.experimental import pallas as pl
from jax.experimental.pallas import tpu as pltpu
from jax.sharding import Mesh, PartitionSpec as P

ROOT_THREE = math.sqrt(3.0)
SCALE_NORM = 4.0 * math.sqrt(2.0)
LOW_PASS = (
    (1.0 + ROOT_THREE) / SCALE_NORM,
    (3.0 + ROOT_THREE) / SCALE_NORM,
    (3.0 - ROOT_THREE) / SCALE_NORM,
    (1.0 - ROOT_THREE) / SCALE_NORM,
)
HIGH_PASS = (LOW_PASS[3], -LOW_PASS[2], LOW_PASS[1], -LOW_PASS[0])

NY, NZ, NC, NR = 4, 16, 2, 4
FINE = ("y", "zhigh", "zmid", "zlow", "core")
EVERY = FINE + ("rep",)
NH, NM, NL = 4, 2, 2
BS = 128
BLOCKS_HERE = 48
MARGIN = BLOCKS_HERE // 4
WINDOW = BLOCKS_HERE + 2 * MARGIN
BLOCKS_ALL = BLOCKS_HERE * NY * NZ * NC
LOWS = BLOCKS_HERE // 2
SLOTS = NH * NM * NC * 2
PORTS_DEV = 8
PORTS = PORTS_DEV * NR
NNZ = 128
UP_ROWS = MARGIN + 2
VMEM = pl.BlockSpec(memory_space=pltpu.VMEM)
SMEM = pl.BlockSpec(memory_space=pltpu.SMEM)
PARAMS = pltpu.CompilerParams(vmem_limit_bytes=48 * 1024 * 1024)


def inverse_matrix():
    taps = np.zeros((2 * BS, 2 * BS), np.float32)
    for k in range(BS):
        for odd in range(2):
            taps[k, 2 * k + odd] = LOW_PASS[odd]
            taps[BS + k, 2 * k + odd] = HIGH_PASS[odd]
            if k:
                taps[k - 1, 2 * k + odd] = LOW_PASS[2 + odd]
                taps[BS + k - 1, 2 * k + odd] = HIGH_PASS[2 + odd]
    return taps


def dot_exact(a, b):
    return jnp.dot(a, b, precision=lax.Precision.HIGHEST, preferred_element_type=jnp.float32)


def forward_kernel(x_ref, asked_ref, out_ref, wanted_ref):
    asked = jnp.maximum(asked_ref[...], 0)
    for i in range(NY * NL * NR):
        wanted_ref[i] = asked
    wide = 2 * BS
    row = lax.broadcasted_iota(jnp.int32, (wide + BS, wide), 0)
    lane = lax.broadcasted_iota(jnp.int32, (wide + BS, wide), 1)
    is_low = lane < BS
    tap = row - 2 * jnp.where(is_low, lane, lane - BS)
    taps = jnp.zeros((wide + BS, wide), jnp.float32)
    for j in range(4):
        taps = jnp.where(tap == j, jnp.where(is_low, LOW_PASS[j], HIGH_PASS[j]), taps)
    here = jnp.concatenate(
        [x_ref[:, wide * b : wide * (b + 1)] for b in range(LOWS)], axis=0
    )
    after = jnp.concatenate(
        [x_ref[:, wide * b : wide * b + BS] for b in range(1, LOWS)]
        + [jnp.zeros((PORTS_DEV, BS), jnp.float32)],
        axis=0,
    )
    bands = dot_exact(here, taps[:wide]) + dot_exact(after, taps[wide:])
    for b in range(BLOCKS_HERE):
        rows = PORTS_DEV * (b % LOWS)
        lanes = BS * (b // LOWS)
        out_ref[b] = bands[rows : rows + PORTS_DEV, lanes : lanes + BS]


def finish_kernel(bands_ref, next_ref, out_ref):
    lane = lax.broadcasted_iota(jnp.int32, (PORTS_DEV, BS), 1)
    for b in range(BLOCKS_HERE):
        band = bands_ref[b]
        if b % LOWS == LOWS - 1:
            taps = HIGH_PASS if b // LOWS else LOW_PASS
            head = taps[2] * next_ref[:, 0:1] + taps[3] * next_ref[:, 1:2]
            band = band + jnp.where(lane == BS - 1, head, 0.0)
        out_ref[b] = band.astype(jnp.bfloat16)


def select_kernel(wanted_ref, same_ref, other_ref, out_ref):
    middle = lax.axis_index("zmid")
    corner = (lax.axis_index("y") * NZ + lax.axis_index("zlow")) * NC

    def one(reader, carry):
        for high in range(NH):
            for swap, table_ref in enumerate((same_ref, other_ref)):
                pair = high * NM + (middle ^ swap)
                for core in range(NC):
                    source = corner + pair * NL * NC + core
                    for k in range(2):
                        block = wanted_ref[reader, k, source]
                        slot = (pair * NC + core) * 2 + k
                        out_ref[reader, slot] = table_ref[core, high, block]
        return carry

    lax.fori_loop(0, NY * NL * NR, one, 0)


def seg_index():
    z = lax.axis_index("zhigh") * NM + lax.axis_index("zmid")
    z = z * NL + lax.axis_index("zlow")
    return (lax.axis_index("y") * NZ + z) * NC + lax.axis_index("core")


def product_kernel(rows_ref, slots_ref, vectors_ref, coupling_ref, total_ref, near_ref, far_ref):
    edge = seg_index() * BLOCKS_HERE - MARGIN
    total_ref[...] = jnp.zeros_like(total_ref)
    for n in range(NNZ):
        row = rows_ref[0, n] - edge
        row = jnp.where(row < 0, row + BLOCKS_ALL, row)
        row = jnp.where(row >= BLOCKS_ALL, row - BLOCKS_ALL, row)
        slot = slots_ref[0, n]
        source = slot >> 1
        z = (source >> 1) & (NZ - 1)
        place = (z >> 1) * NC * 2 + (slot & 3)
        vector = jnp.concatenate(
            [vectors_ref[r, z & 1, source >> 5, place] for r in range(NR)], axis=0
        )
        product = lax.dot_general(
            vector,
            coupling_ref[n],
            (((1,), (1,)), ((), ())),
            preferred_element_type=jnp.float32,
        )
        total_ref[row] += product

    def margins(up_ref, down_ref):
        down_ref[:MARGIN] = total_ref[:MARGIN].astype(jnp.bfloat16)
        down_ref[MARGIN:] = jnp.zeros((2, PORTS, BS), jnp.bfloat16)
        up_ref[:MARGIN] = total_ref[MARGIN + BLOCKS_HERE :].astype(jnp.bfloat16)
        up_ref[MARGIN] = total_ref[MARGIN + LOWS - 1].astype(jnp.bfloat16)
        up_ref[MARGIN + 1] = total_ref[MARGIN + BLOCKS_HERE - 1].astype(jnp.bfloat16)

    core = lax.axis_index("core")
    pl.when(core == 0)(lambda: margins(near_ref, far_ref))
    pl.when(core == 1)(lambda: margins(far_ref, near_ref))


def combine_kernel(total_ref, nears_ref, far_ref, out_ref):
    def combine(above_ref, below_ref):
        for row in range(BLOCKS_HERE + 2):
            if row < BLOCKS_HERE:
                value = total_ref[MARGIN + row]
                if row < MARGIN:
                    value = value + above_ref[row].astype(jnp.float32)
                if row >= BLOCKS_HERE - MARGIN:
                    value = value + below_ref[row - BLOCKS_HERE + MARGIN].astype(jnp.float32)
            else:
                value = above_ref[MARGIN + row - BLOCKS_HERE].astype(jnp.float32)
                if row == BLOCKS_HERE + 1:
                    value = value + total_ref[MARGIN - 1]
            for r in range(NR):
                out_ref[r, row] = value[PORTS_DEV * r : PORTS_DEV * (r + 1)].astype(jnp.bfloat16)

    core = lax.axis_index("core")
    pl.when(core == 0)(lambda: combine(far_ref, nears_ref.at[1]))
    pl.when(core == 1)(lambda: combine(nears_ref.at[0], far_ref))


def inverse_kernel(parts_ref, taps_ref, out_ref):
    rows = parts_ref[0].astype(jnp.float32)
    for r in range(1, NR):
        rows = rows + parts_ref[r].astype(jnp.float32)
    flat = LOWS * PORTS_DEV
    low = rows[:LOWS].reshape(flat, BS)
    high = rows[LOWS:BLOCKS_HERE].reshape(flat, BS)
    low_before = jnp.concatenate([rows[BLOCKS_HERE], low[: flat - PORTS_DEV]], axis=0)
    high_before = jnp.concatenate([rows[BLOCKS_HERE + 1], high[: flat - PORTS_DEV]], axis=0)
    volts = dot_exact(jnp.concatenate([low, high], axis=1), taps_ref[...])
    low_last, high_last = low_before[:, BS - 1 :], high_before[:, BS - 1 :]
    lane = lax.broadcasted_iota(jnp.int32, (flat, BS), 1)
    edge = jnp.where(lane == 0, LOW_PASS[2] * low_last + HIGH_PASS[2] * high_last, 0.0)
    edge = jnp.where(lane == 1, LOW_PASS[3] * low_last + HIGH_PASS[3] * high_last, edge)
    near_edge = volts[:, :BS] + edge
    for b in range(LOWS):
        rows = slice(PORTS_DEV * b, PORTS_DEV * (b + 1))
        out_ref[:, 2 * BS * b : 2 * BS * b + BS] = near_edge[rows]
        out_ref[:, 2 * BS * b + BS : 2 * BS * (b + 1)] = volts[rows, BS:]


def route(block, partner):
    count = NY * NZ * NC
    return lax.ppermute(block, FINE, [(i, partner(i) % count) for i in range(count)])


def windows():
    groups = []
    for core in range(NC):
        for even in range(0, NZ, 2):
            odd = (even + 1 - 2 * core) % NZ
            groups.append(
                [
                    ((y * NZ + z) * NC + core) * NR + r
                    for r in range(NR)
                    for z in (even, odd)
                    for y in range(NY)
                ]
            )
    return groups


def two_away(i):
    core, z, y = i % NC, i // NC % NZ, i // (NC * NZ)
    step = 2 if (z >> 1) % 2 == core else -2
    return (y * NZ + (z + step) % NZ) * NC + core


def to_window(block):
    return lax.all_to_all(block, EVERY, 0, 0, tiled=True, axis_index_groups=windows())


def shards(currents, requested, block_rows, block_slots, coupling):
    bf16 = jnp.bfloat16
    next_head = route(currents[:, :BS], lambda i: i - 1)
    bands, wanted = pl.pallas_call(
        forward_kernel,
        out_shape=[
            jax.ShapeDtypeStruct((BLOCKS_HERE, PORTS_DEV, BS), jnp.float32),
            jax.ShapeDtypeStruct((NY * NL * NR,) + requested.shape[:1:-1], jnp.int32),
        ],
        in_specs=[VMEM, VMEM],
        out_specs=[VMEM, VMEM],
        compiler_params=PARAMS,
        name="forward",
    )(currents, requested[0, 0].T)
    same = pl.pallas_call(
        finish_kernel,
        out_shape=jax.ShapeDtypeStruct((BLOCKS_HERE, PORTS_DEV, BS), bf16),
        in_specs=[VMEM, VMEM],
        out_specs=VMEM,
        compiler_params=PARAMS,
        name="finish",
    )(bands, next_head)
    same = lax.all_gather(same, "zhigh", axis=0)
    same, wanted = lax.optimization_barrier((same, wanted))
    other = route(same, two_away)
    same = lax.all_gather(same, "core", axis=0)
    wanted = to_window(wanted)
    other = lax.all_gather(other, "core", axis=0)
    chosen = pl.pallas_call(
        select_kernel,
        out_shape=jax.ShapeDtypeStruct((NY * NL * NR, SLOTS, PORTS_DEV, BS), bf16),
        in_specs=[SMEM, VMEM, VMEM],
        out_specs=VMEM,
        compiler_params=PARAMS,
        name="select",
    )(wanted, same, other)
    vectors = to_window(chosen).reshape(NR, NL, NY, SLOTS, PORTS_DEV, BS)
    total, near, far = pl.pallas_call(
        product_kernel,
        out_shape=[
            jax.ShapeDtypeStruct((WINDOW, PORTS, BS), jnp.float32),
            jax.ShapeDtypeStruct((UP_ROWS, PORTS, BS), bf16),
            jax.ShapeDtypeStruct((UP_ROWS, PORTS, BS), bf16),
        ],
        in_specs=[SMEM, SMEM, VMEM, VMEM],
        out_specs=[VMEM, VMEM, VMEM],
        compiler_params=pltpu.CompilerParams(vmem_limit_bytes=24 * 1024 * 1024),
        name="products",
    )(block_rows[0], block_slots[0], vectors, coupling[0, 0])
    nears = lax.all_gather(near, "core", axis=0)
    far = route(far, lambda i: i + 1 if i % 2 else i - 1)
    parts = pl.pallas_call(
        combine_kernel,
        out_shape=jax.ShapeDtypeStruct((NR, BLOCKS_HERE + 2, PORTS_DEV, BS), bf16),
        in_specs=[VMEM, VMEM, VMEM],
        out_specs=VMEM,
        compiler_params=PARAMS,
        name="combine",
    )(total, nears, far)
    parts = lax.all_to_all(parts, "rep", 0, 0, tiled=True)
    return pl.pallas_call(
        inverse_kernel,
        out_shape=jax.ShapeDtypeStruct(currents.shape, jnp.float32),
        in_specs=[VMEM, VMEM],
        out_specs=VMEM,
        compiler_params=PARAMS,
        name="inverse",
    )(parts, jnp.asarray(inverse_matrix()))


def solution(mesh):
    grid = Mesh(mesh.devices.reshape(NY, NH, NM, NL, NC, NR), EVERY)
    placed = (
        P("rep", FINE),
        P(FINE, "rep", None, None),
        P(FINE, "rep", None),
        P(FINE, "rep", None),
        P(FINE, "rep", None, None, None),
    )
    return jax.shard_map(
        shards, mesh=grid, in_specs=placed, out_specs=P("rep", FINE), check_vma=False
    )
```
